32 devices in a mesh: prow: 16 (over z, y, x), pcol: 2 (over core).
Axes of the slice: x: 2, y: 2, z: 4, core: 2. Of those that a mesh axis runs over, the one named last changes fastest.
Arguments:
- trailing: float32 [8192, 8192], P('prow', 'pcol'), may hold values from -48 to 48, as said below
- panel: float32 [8192, 256], P('prow', 'pcol'), may hold values from -48 to 48, as said below
Outputs:
- updated: float32 [8192, 8192], P('prow', 'pcol')
- basis_out: float32 [8192, 256], P('prow')
The draws below stay inside these ranges and needn't reach their ends.
Inputs may be any that keep to these rules, and one draw needn't show every extreme that they name: trailing is exactly symmetric, with a positive added diagonal. panel has full column rank.
All inputs are finite; a program needn't handle non-finite values.
Results may differ from the reference program's by a relative error of at most 0.000096.
Values sent between devices are 32-bit elements; how exact they have to be, the bound alone decides.
A program may use at most 64 MiB of HBM per device.

```python
import math
import jax
import jax.numpy as jnp
from jax import lax

PANEL = 256
ORDER = 8192


def draw_trailing(key, part):
    key = jax.random.fold_in(key, 11)
    noise_key = jax.random.fold_in(key, 0)
    noise = jax.random.normal(noise_key, (ORDER, ORDER), jnp.float32)
    symmetric = (noise + noise.T) * math.sqrt(0.5)
    index_rows = lax.broadcasted_iota(jnp.int32, (ORDER, ORDER), 0)
    index_cols = lax.broadcasted_iota(jnp.int32, (ORDER, ORDER), 1)
    diagonal = jnp.where(index_rows == index_cols, 4.0, 0.0).astype(jnp.float32)
    return jnp.clip(symmetric + diagonal, -48.0, 48.0)


def draw_panel(key, part):
    key = jax.random.fold_in(key, 23)
    noise_key = jax.random.fold_in(key, 0)
    values = jax.random.normal(noise_key, (ORDER, PANEL), jnp.float32)
    return jnp.clip(values, -48.0, 48.0)


def setup_inputs(seed: int = 0) -> dict:
    keys = jax.random.split(jax.random.key(seed), 3)
    return {
        "trailing": draw_trailing(jax.random.fold_in(keys[2], 71), 0),
        "panel": draw_panel(jax.random.fold_in(keys[2], 71), 0),
    }


def matmul(left, right):
    return jnp.dot(left.astype(jnp.float32), right.astype(jnp.float32), precision=lax.Precision.HIGHEST, preferred_element_type=jnp.float32)

def reference(trailing, panel):
    gram = matmul(panel.T, panel)
    factor = jnp.linalg.cholesky(gram)
    basis_out = lax.linalg.triangular_solve(factor, panel, left_side=False, lower=True, transpose_a=True)
    product = matmul(trailing, basis_out)
    projected = matmul(basis_out.T, product)
    correction = product - 0.5 * matmul(basis_out, projected)
    updated = trailing - matmul(basis_out, correction.T) - matmul(correction, basis_out.T)
    return (updated, basis_out)
```

```python
import functools
import jax
import jax.numpy as jnp
from jax import lax
from jax.experimental import pallas as pl
from jax.experimental.pallas import tpu as pltpu
from jax.sharding import PartitionSpec as P

MESH = pl.DeviceIdType.MESH
SUB = 8
PLANE = 4


def matmul(left, right):
    return jnp.dot(left, right, precision=lax.Precision.HIGHEST, preferred_element_type=jnp.float32)


def dot_exact(left, right, dims):
    return lax.dot_general(
        left, right, (dims, ((), ())), precision=lax.Precision.HIGHEST,
        preferred_element_type=jnp.float32,
    )


def split(value):
    high = value.astype(jnp.bfloat16)
    low = (value - high.astype(jnp.float32)).astype(jnp.bfloat16)
    return high, low


def dot_split(left, right, dims):
    dot = functools.partial(
        lax.dot_general, dimension_numbers=(dims, ((), ())), preferred_element_type=jnp.float32
    )
    (left_high, left_low), (right_high, right_low) = left, right
    return dot(left_high, right_high) + (dot(left_high, right_low) + dot(left_low, right_high))


NN = ((1,), (0,))
NT = ((1,), (1,))
TN = ((0,), (0,))


def factor_rows(index, work, inverse):
    width = inverse.shape[1]
    start = pl.multiple_of(index * SUB, SUB)
    rows = work[pl.ds(start, SUB), :]
    lane = lax.broadcasted_iota(jnp.int32, (SUB, width), 1)
    sub = lax.broadcasted_iota(jnp.int32, (SUB, 128), 0)
    diagonal = [
        jnp.broadcast_to(
            jnp.sum(jnp.where(lane == start + i, rows[:, :width], 0.0), axis=1, keepdims=True),
            (SUB, 128),
        )
        for i in range(SUB)
    ]
    unit = [jnp.where(sub == i, 1.0, 0.0).astype(jnp.float32) for i in range(SUB)]
    scale = jnp.zeros((SUB, 128), jnp.float32)
    for i in range(SUB):
        pivot = jnp.broadcast_to(diagonal[i][i : i + 1, :], (SUB, 128))
        root = lax.rsqrt(pivot)
        root = root * (1.5 - 0.5 * (pivot * root) * root)
        scale = jnp.where(sub == i, root, scale)
        if i + 1 < SUB:
            ratio = jnp.where(sub > i, (diagonal[i] * root) * root, 0.0)
            for k in range(i + 1, SUB):
                diagonal[k] = diagonal[k] - ratio * diagonal[k][i : i + 1, :]
            for k in range(i + 1):
                unit[k] = unit[k] - ratio * unit[k][i : i + 1, :]
    reduced = jnp.zeros_like(rows)
    for i in range(SUB):
        weight = jnp.concatenate([scale * unit[i]] * (rows.shape[1] // 128), 1)
        reduced = reduced + weight * rows[i : i + 1, :]
    inverse[pl.ds(start, SUB), :] = reduced[:, width:]
    work[...] = work[...] - dot_exact(reduced[:, :width], reduced, TN)


def kernel(planes, trailing, panel, updated, basis_out, held, pblocks, wblocks, partial, wrecv,
           gram, grecv, proj, hrecv, work, inverse, xrows, zrows,
           load_sem, store_sem, basis_sem, pz, p1, p2, ps, precv, psib, wz, w1, w2, ws, wr, wsib,
           swap_send, swap_recv):
    row, col = lax.axis_index("prow"), lax.axis_index("pcol")
    height, half = panel.shape
    width = 2 * half
    depth = row // PLANE
    place = lax.rem(row, PLANE)
    stride1 = 2 - col
    stride2 = 1 + col
    flip1 = stride1 * (1 - 2 * lax.rem(place // stride1, 2))
    flip2 = stride2 * (1 - 2 * lax.rem(place // stride2, 2))
    other = 1 - col
    near = planes // 2

    def plane_of(k):
        return lax.rem(depth + k, planes)

    load = pltpu.make_async_copy(trailing, held, load_sem)
    load.start()
    barrier = pltpu.get_barrier_semaphore()
    peers = [(plane_of(k) * PLANE + place, col) for k in range(1, planes)]
    peers += [(row + flip1, col), (row + flip2, col), (row, other)]
    for peer in peers:
        pl.semaphore_signal(barrier, inc=1, device_id=peer, device_id_type=MESH)
    pl.semaphore_wait(barrier, len(peers))

    class Gather:
        def __init__(self, blocks, sends, recv, sib):
            self.blocks, self.recv, self.sib = blocks, recv, sib
            self.sz, self.s1, self.s2, self.ss = sends

        def copy(self, block, sem, recv, to, src=None):
            ref = self.blocks.at[col, block]
            return pltpu.make_async_remote_copy(
                src_ref=ref, dst_ref=ref, send_sem=sem, recv_sem=recv.at[block],
                device_id=to, device_id_type=MESH,
            )

        def zcopy(self, k):
            return self.copy(row, self.sz.at[k], self.recv, (plane_of(k) * PLANE + place, col))

        def copy1(self, k):
            return self.copy(plane_of(k) * PLANE + place, self.s1.at[k], self.recv,
                             (row + flip1, col))

        def copy2(self, k, hop):
            return self.copy(plane_of(k) * PLANE + place + hop * flip1, self.s2.at[k, hop],
                             self.recv, (row + flip2, col))

        def copys(self, block):
            return self.copy(block, self.ss.at[block], self.sib, (row, other))

        def arrived(self, block):
            self.copy(block, self.sz.at[0], self.recv, (row, other)).wait_recv()

        def sibling_arrived(self, block):
            ref = self.blocks.at[other, block]
            pltpu.make_async_remote_copy(
                src_ref=ref, dst_ref=ref, send_sem=self.sz.at[0], recv_sem=self.sib.at[block],
                device_id=(row, other), device_id_type=MESH,
            ).wait_recv()

        def first(self):
            self.copys(row).start()
            self.copy1(0).start()
            self.copy2(0, 0).start()
            for k in range(1, planes):
                self.zcopy(k).start()

        def forward0(self, k):
            self.arrived(plane_of(k) * PLANE + place)
            self.copy1(k).start()
            self.copy2(k, 0).start()

        def forward1(self, k):
            self.arrived(plane_of(k) * PLANE + place + flip1)
            self.copy2(k, 1).start()

        def forward2(self, k):
            for hop in range(2):
                self.arrived(plane_of(k) * PLANE + place + flip2 + hop * flip1)

            @pl.when(plane_of(k) // near != col)
            def _():
                for b in range(PLANE):
                    block = plane_of(k) * PLANE + b
                    if k:
                        self.copys(block).start()
                    else:
                        @pl.when(block != row)
                        def _():
                            self.copys(block).start()

        def sibling(self, k):
            for b in range(PLANE):
                block = plane_of(k) * PLANE + b
                if k:
                    self.sibling_arrived(block)
                else:
                    @pl.when(block != row)
                    def _():
                        self.sibling_arrived(block)

        def steps(self):
            order = [0]
            for k in range(1, planes // 2 + 1):
                order += [k] if 2 * k == planes else [k, planes - k]
            out = []
            for t in range(planes + 2):
                for lag, step in ((0, self.forward0), (1, self.forward1), (2, self.forward2)):
                    if 0 <= t - lag < planes and (lag or t):
                        out.append((step, order[t - lag]))
            return out, order

        def finish(self):
            self.copys(row).wait_send()
            for k in range(planes):
                if k:
                    self.zcopy(k).wait_send()
                self.copy1(k).wait_send()
                for hop in range(2):
                    self.copy2(k, hop).wait_send()

                @pl.when(plane_of(k) // near != col)
                def _():
                    for b in range(PLANE):
                        block = plane_of(k) * PLANE + b
                        if k:
                            self.copys(block).wait_send()
                        else:
                            @pl.when(block != row)
                            def _():
                                self.copys(block).wait_send()

    def full(blocks, block):
        return jnp.concatenate([blocks[0, block], blocks[1, block]], 1)

    def swap(source, target, slot):
        return pltpu.make_async_remote_copy(
            src_ref=source, dst_ref=target, send_sem=swap_send.at[slot],
            recv_sem=swap_recv.at[slot], device_id=(row, other), device_id_type=MESH,
        )

    pgather = Gather(pblocks, (pz, p1, p2, ps), precv, psib)
    pblocks[col, row] = panel[...]
    pgather.first()
    partial[...] = jnp.zeros_like(partial)
    gram[...] = jnp.zeros_like(gram)
    load.wait()
    steps, order = pgather.steps()
    pgather.sibling_arrived(row)

    def multiply(k):
        @pl.when(plane_of(k) // near == col)
        def _():
            pgather.sibling(k)

            @pl.loop(0, PLANE)
            def _(b):
                block = plane_of(k) * PLANE + b
                columns = pl.ds(pl.multiple_of((block - col * near * PLANE) * height, height), height)
                values = full(pblocks, block)
                product = dot_split(split(held[:, columns]), split(values), NN)
                partial[0] += product[:, :half]
                partial[1] += product[:, half:]
                gram[...] += dot_exact(values, values, TN)

    for step, k in steps:
        step(k)
        if step == pgather.forward2:
            multiply(k)

    wswap = swap(partial.at[other], wrecv, 0)
    wswap.start()
    gswap = swap(gram, grecv, 1)
    gswap.start()
    wswap.wait()
    wblocks[col, row] = partial[col] + wrecv[...]
    wgather = Gather(wblocks, (wz, w1, w2, ws), wr, wsib)
    wgather.first()
    gswap.wait()
    work[:, :width] = gram[...] + grecv[...]
    work[:, width:] = jnp.where(
        lax.broadcasted_iota(jnp.int32, (width, width), 0)
        == lax.broadcasted_iota(jnp.int32, (width, width), 1), 1.0, 0.0)

    wsteps, _ = wgather.steps()
    count = width // SUB
    bounds = [count * (i + 1) // (len(wsteps) + 1) for i in range(len(wsteps) + 1)]
    begin = 0
    for i, end in enumerate(bounds):
        lax.fori_loop(begin, end, lambda j, _: (factor_rows(j, work, inverse), 0)[1], 0)
        begin = end
        if i < len(wsteps):
            step, k = wsteps[i]
            step(k)

    linv = inverse[...]
    basis = dot_exact(full(pblocks, row), linv, NT)
    gram_basis = dot_exact(basis, linv, NN)
    xrows[...] = gram_basis
    zrows[...] = basis
    basis_copy = pltpu.make_async_copy(zrows, basis_out, basis_sem)
    basis_copy.start()
    proj[...] = jnp.zeros_like(proj)
    wgather.sibling_arrived(row)

    def column_update(k):
        @pl.when(plane_of(k) // near == col)
        def _():
            wgather.sibling(k)

            @pl.loop(0, PLANE)
            def _(b):
                block = plane_of(k) * PLANE + b
                columns = pl.ds(pl.multiple_of((block - col * near * PLANE) * height, height), height)
                values = full(wblocks, block)
                held[:, columns] -= dot_split(split(xrows[...]), split(values), NT)
                proj[...] += dot_exact(full(pblocks, block), values, TN)

    for k in order:
        column_update(k)
    hswap = swap(proj, hrecv, 2)
    hswap.start()
    hswap.wait()
    total = proj[...] + hrecv[...]
    rest = full(wblocks, row) - dot_exact(xrows[...], total, NN)
    basis_copy.wait()
    zrows[...] = dot_exact(dot_exact(rest, linv, NT), linv, NN)
    blocks = near * PLANE
    stores = []
    for b in range(blocks):
        columns = pl.ds(b * height, height)
        values = full(pblocks, col * blocks + b)
        held[:, columns] -= dot_split(split(zrows[...]), split(values), NT)
        store = pltpu.make_async_copy(held.at[:, columns], updated.at[:, columns], store_sem.at[b])
        store.start()
        stores.append(store)
    pgather.finish()
    wgather.finish()
    for store in stores:
        store.wait()


def fused(trailing, panel, rows, interpret=False):
    height, half = panel.shape
    width = 2 * half
    planes = rows // PLANE
    blocks = (2, rows, height, half)
    dma = pltpu.SemaphoreType.DMA
    vmem = lambda *shape: pltpu.VMEM(shape, jnp.float32)
    gather_sems = [dma((planes,)), dma((planes,)), dma((planes, 2)), dma((rows,)), dma((rows,)),
                   dma((rows,))]
    return pl.pallas_call(
        functools.partial(kernel, planes),
        out_shape=(jax.ShapeDtypeStruct(trailing.shape, jnp.float32),
                   jax.ShapeDtypeStruct((height, width), jnp.float32)),
        in_specs=[pl.BlockSpec(memory_space=pl.ANY), pl.BlockSpec(memory_space=pltpu.VMEM)],
        out_specs=[pl.BlockSpec(memory_space=pl.ANY), pl.BlockSpec(memory_space=pl.ANY)],
        scratch_shapes=[
            vmem(*trailing.shape), vmem(*blocks), vmem(*blocks), vmem(2, height, half),
            vmem(height, half), vmem(width, width), vmem(width, width), vmem(width, width),
            vmem(width, width), vmem(width, 2 * width), vmem(width, width), vmem(height, width),
            vmem(height, width),
            dma, dma((rows // 2,)), dma, *gather_sems, *gather_sems, dma((3,)), dma((3,)),
        ],
        compiler_params=pltpu.CompilerParams(
            collective_id=0, has_side_effects=True, vmem_limit_bytes=56 * 2**20
        ),
        name="panel_update",
    )(trailing, panel)


def shards(trailing, panel):
    rows, cols = lax.axis_size("prow"), lax.axis_size("pcol")
    if cols == 2 and rows % (2 * PLANE) == 0 and panel.shape[1] % 128 == 0:
        return tuple(fused(trailing, panel, rows))
    gather = lambda value: lax.all_to_all(
        lax.all_gather(value, "prow", axis=0, tiled=True), "pcol", 0, 1, tiled=True
    )
    panel_rows = lax.all_gather(panel, "pcol", axis=1, tiled=True)
    panel_cols = gather(panel)
    gram = lax.psum(matmul(panel_cols.T, panel_cols), "pcol")
    factor = jnp.linalg.cholesky(gram)
    solve = functools.partial(
        lax.linalg.triangular_solve, factor, left_side=False, lower=True, transpose_a=True
    )
    basis_rows, basis_cols = solve(panel_rows), solve(panel_cols)
    part = lax.psum_scatter(
        matmul(trailing, basis_cols), "pcol", scatter_dimension=1, tiled=True
    )
    product_rows = lax.all_gather(part, "pcol", axis=1, tiled=True)
    product_cols = gather(part)
    projected = lax.psum(matmul(basis_cols.T, product_cols), "pcol")
    correction = product_rows - 0.5 * matmul(basis_rows, projected)
    correction_cols = product_cols - 0.5 * matmul(basis_cols, projected)
    updated = trailing - matmul(basis_rows, correction_cols.T) - matmul(correction, basis_cols.T)
    return (updated, basis_rows)


def solution(mesh):
    in_specs = (P("prow", "pcol"), P("prow", "pcol"))
    out_specs = (P("prow", "pcol"), P("prow", None))
    return jax.shard_map(shards, mesh=mesh, in_specs=in_specs, out_specs=out_specs, check_vma=False)
```

```python
import functools
import jax
import jax.numpy as jnp
from jax import lax
from jax.experimental import pallas as pl
from jax.experimental.pallas import tpu as pltpu
from jax.sharding import PartitionSpec as P

MESH = pl.DeviceIdType.MESH
SUB = 8
PLANE = 4
BLOCK = 128


def matmul(left, right):
    return jnp.dot(left, right, precision=lax.Precision.HIGHEST, preferred_element_type=jnp.float32)


def dot_exact(left, right, dims):
    return lax.dot_general(
        left, right, (dims, ((), ())), precision=lax.Precision.HIGHEST,
        preferred_element_type=jnp.float32,
    )


def split(value):
    high = value.astype(jnp.bfloat16)
    low = (value - high.astype(jnp.float32)).astype(jnp.bfloat16)
    return high, low


def dot_split(left, right, dims):
    dot = functools.partial(
        lax.dot_general, dimension_numbers=(dims, ((), ())), preferred_element_type=jnp.float32
    )
    (left_high, left_low), (right_high, right_low) = left, right
    return dot(left_high, right_high) + (dot(left_high, right_low) + dot(left_low, right_high))


NN = ((1,), (0,))
NT = ((1,), (1,))
TN = ((0,), (0,))


def factor_rows(index, lo, work, upper):
    hi = lo + upper.shape[1] // 2 + BLOCK
    start = pl.multiple_of(index * SUB, SUB)
    rows = work[pl.ds(start, SUB), lo:hi]
    lane = lax.broadcasted_iota(jnp.int32, (SUB, BLOCK), 1)
    sub = lax.broadcasted_iota(jnp.int32, (SUB, BLOCK), 0)
    diagonal = [
        jnp.broadcast_to(
            jnp.sum(jnp.where(lane == start - lo + i, rows[:, :BLOCK], 0.0), axis=1, keepdims=True),
            (SUB, BLOCK),
        )
        for i in range(SUB)
    ]
    unit = [jnp.where(sub == i, 1.0, 0.0).astype(jnp.float32) for i in range(SUB)]
    pivots = diagonal[0]
    for i in range(SUB):
        pivots = jnp.where(sub == i, diagonal[i], pivots)
        if i + 1 < SUB:
            pivot = jnp.broadcast_to(diagonal[i][i : i + 1, :], (SUB, BLOCK))
            ratio = jnp.where(sub > i, diagonal[i], 0.0) * pl.reciprocal(pivot)
            for k in range(i + 1, SUB):
                diagonal[k] = diagonal[k] - ratio * diagonal[k][i : i + 1, :]
            for k in range(i + 1):
                unit[k] = unit[k] - ratio * unit[k][i : i + 1, :]
    scale = lax.rsqrt(pivots)
    scale = scale * (1.5 - 0.5 * (pivots * scale) * scale)
    reduced = jnp.zeros_like(rows)
    for i in range(SUB):
        weight = jnp.concatenate([scale * unit[i]] * (rows.shape[1] // BLOCK), 1)
        reduced = reduced + weight * rows[i : i + 1, :]
    upper[pl.ds(start, SUB), lo:hi] = reduced
    high = reduced.astype(jnp.bfloat16).astype(jnp.float32)
    rest = reduced - high
    mid = rest.astype(jnp.bfloat16).astype(jnp.float32)
    low = rest - mid
    left = jnp.concatenate([part[:, :BLOCK] for part in (high, high, mid, high, low, mid)], 0)
    right = jnp.concatenate([high, mid, high, low, high, mid], 0)
    work[lo : lo + BLOCK, lo:hi] -= lax.dot_general(
        left.astype(jnp.bfloat16), right.astype(jnp.bfloat16), (TN, ((), ())),
        preferred_element_type=jnp.float32,
    )


def factor_below(lo, work, upper):
    width = upper.shape[1] // 2
    mid, hi = lo + BLOCK, lo + width + BLOCK
    if mid < width:
        work[mid:, mid:hi] -= dot_exact(upper[lo:mid, mid:width], upper[lo:mid, mid:hi], TN)


def kernel(planes, trailing, panel, pcols, wcols, rowside, basis_out, held, pblocks, wblocks,
           partial, wrecv, gram, grecv, proj, hrecv, work, upper, load_sem, store_sem, pz, p1, p2, ps, precv, psib, wz, w1, w2, ws, wr, wsib,
           swap_send, swap_recv):
    row, col = lax.axis_index("prow"), lax.axis_index("pcol")
    height, half = panel.shape
    width = 2 * half
    depth = row // PLANE
    place = lax.rem(row, PLANE)
    stride1 = 2 - col
    stride2 = 1 + col
    flip1 = stride1 * (1 - 2 * lax.rem(place // stride1, 2))
    flip2 = stride2 * (1 - 2 * lax.rem(place // stride2, 2))
    other = 1 - col
    near = planes // 2

    def plane_of(k):
        return lax.rem(depth + k, planes)

    load = pltpu.make_async_copy(trailing, held, load_sem)
    load.start()
    barrier = pltpu.get_barrier_semaphore()
    peers = [(plane_of(k) * PLANE + place, col) for k in range(1, planes)]
    peers += [(row + flip1, col), (row + flip2, col), (row, other)]
    for peer in peers:
        pl.semaphore_signal(barrier, inc=1, device_id=peer, device_id_type=MESH)
    pl.semaphore_wait(barrier, len(peers))

    class Gather:
        def __init__(self, blocks, sends, recv, sib):
            self.blocks, self.recv, self.sib = blocks, recv, sib
            self.sz, self.s1, self.s2, self.ss = sends

        def copy(self, block, sem, recv, to, src=None):
            ref = self.blocks.at[col, block]
            return pltpu.make_async_remote_copy(
                src_ref=ref, dst_ref=ref, send_sem=sem, recv_sem=recv.at[block],
                device_id=to, device_id_type=MESH,
            )

        def zcopy(self, k):
            return self.copy(row, self.sz.at[k], self.recv, (plane_of(k) * PLANE + place, col))

        def copy1(self, k):
            return self.copy(plane_of(k) * PLANE + place, self.s1.at[k], self.recv,
                             (row + flip1, col))

        def copy2(self, k, hop):
            return self.copy(plane_of(k) * PLANE + place + hop * flip1, self.s2.at[k, hop],
                             self.recv, (row + flip2, col))

        def copys(self, block):
            return self.copy(block, self.ss.at[block], self.sib, (row, other))

        def arrived(self, block):
            self.copy(block, self.sz.at[0], self.recv, (row, other)).wait_recv()

        def sibling_arrived(self, block):
            ref = self.blocks.at[other, block]
            pltpu.make_async_remote_copy(
                src_ref=ref, dst_ref=ref, send_sem=self.sz.at[0], recv_sem=self.sib.at[block],
                device_id=(row, other), device_id_type=MESH,
            ).wait_recv()

        def first(self):
            self.copys(row).start()
            self.copy1(0).start()
            self.copy2(0, 0).start()
            for k in range(1, planes):
                self.zcopy(k).start()

        def forward0(self, k):
            self.arrived(plane_of(k) * PLANE + place)
            self.copy1(k).start()
            self.copy2(k, 0).start()

        def forward1(self, k):
            self.arrived(plane_of(k) * PLANE + place + flip1)
            self.copy2(k, 1).start()

        def forward2(self, k):
            for hop in range(2):
                self.arrived(plane_of(k) * PLANE + place + flip2 + hop * flip1)

            @pl.when(plane_of(k) // near != col)
            def _():
                for b in range(PLANE):
                    block = plane_of(k) * PLANE + b
                    if k:
                        self.copys(block).start()
                    else:
                        @pl.when(block != row)
                        def _():
                            self.copys(block).start()

        def sibling(self, k):
            for b in range(PLANE):
                block = plane_of(k) * PLANE + b
                if k:
                    self.sibling_arrived(block)
                else:
                    @pl.when(block != row)
                    def _():
                        self.sibling_arrived(block)

        def steps(self):
            order = [0]
            for k in range(1, planes // 2 + 1):
                order += [k] if 2 * k == planes else [k, planes - k]
            out = []
            for t in range(planes + 2):
                for lag, step in ((0, self.forward0), (1, self.forward1), (2, self.forward2)):
                    if 0 <= t - lag < planes and (lag or t):
                        out.append((step, order[t - lag]))
            return out, order

        def finish(self):
            self.copys(row).wait_send()
            for k in range(planes):
                if k:
                    self.zcopy(k).wait_send()
                self.copy1(k).wait_send()
                for hop in range(2):
                    self.copy2(k, hop).wait_send()

                @pl.when(plane_of(k) // near != col)
                def _():
                    for b in range(PLANE):
                        block = plane_of(k) * PLANE + b
                        if k:
                            self.copys(block).wait_send()
                        else:
                            @pl.when(block != row)
                            def _():
                                self.copys(block).wait_send()

    def full(blocks, block):
        return jnp.concatenate([blocks[0, block], blocks[1, block]], 1)

    def swap(source, target, slot):
        return pltpu.make_async_remote_copy(
            src_ref=source, dst_ref=target, send_sem=swap_send.at[slot],
            recv_sem=swap_recv.at[slot], device_id=(row, other), device_id_type=MESH,
        )

    pgather = Gather(pblocks, (pz, p1, p2, ps), precv, psib)
    pblocks[col, row] = panel[...]
    pgather.first()
    partial[...] = jnp.zeros_like(partial)
    gram[...] = jnp.zeros_like(gram)
    load.wait()
    steps, order = pgather.steps()
    pgather.sibling_arrived(row)

    def multiply(k):
        @pl.when(plane_of(k) // near == col)
        def _():
            pgather.sibling(k)

            @pl.loop(0, PLANE)
            def _(b):
                block = plane_of(k) * PLANE + b
                columns = pl.ds(pl.multiple_of((block - col * near * PLANE) * height, height), height)
                values = full(pblocks, block)
                product = dot_split(split(held[:, columns]), split(values), NN)
                partial[0] += product[:, :half]
                partial[1] += product[:, half:]
                gram[...] += dot_exact(values, values, TN)

    for step, k in steps:
        step(k)
        if step == pgather.forward2:
            multiply(k)

    wswap = swap(partial.at[other], wrecv, 0)
    wswap.start()
    gswap = swap(gram, grecv, 1)
    gswap.start()
    wswap.wait()
    wblocks[col, row] = partial[col] + wrecv[...]
    wgather = Gather(wblocks, (wz, w1, w2, ws), wr, wsib)
    wgather.first()
    gswap.wait()
    work[:, :width] = gram[...] + grecv[...]
    work[:, width:] = jnp.where(
        lax.broadcasted_iota(jnp.int32, (width, width), 0)
        == lax.broadcasted_iota(jnp.int32, (width, width), 1), 1.0, 0.0)

    upper[...] = jnp.zeros_like(upper)
    proj[...] = jnp.zeros_like(proj)
    mine = pl.ds(col * near * PLANE, near * PLANE)
    pstore = pltpu.make_async_copy(pblocks.at[:, mine], pcols, store_sem.at[0])
    pstore.start()

    def project(k):
        @pl.when(plane_of(k) // near == col)
        def _():
            wgather.sibling(k)

            @pl.loop(0, PLANE)
            def _(b):
                block = plane_of(k) * PLANE + b
                proj[...] += dot_exact(full(pblocks, block), full(wblocks, block), TN)

    wsteps, _ = wgather.steps()
    for k in order:
        wsteps.insert(wsteps.index((wgather.forward2, k)) + 2, (project, k))
    wsteps.insert(0, (lambda _: wgather.sibling_arrived(row), 0))
    count = BLOCK // SUB
    pieces = 6
    for lo in range(0, width, BLOCK):
        for piece in range(pieces):
            first, last = count * piece // pieces, count * (piece + 1) // pieces
            lax.fori_loop(lo // SUB + first, lo // SUB + last,
                          lambda j, _: (factor_rows(j, lo, work, upper), 0)[1], 0)
            if wsteps:
                step, k = wsteps.pop(0)
                step(k)
        factor_below(lo, work, upper)

    linv = upper[:, width:]
    basis = dot_exact(full(pblocks, row), linv, NT)
    basis_out[...] = basis
    rowside[:, :width] = dot_exact(basis, linv, NN)
    for step, k in wsteps:
        step(k)
    hswap = swap(proj, hrecv, 2)
    hswap.start()
    wstore = pltpu.make_async_copy(wblocks.at[:, mine], wcols, store_sem.at[1])
    wstore.start()
    hswap.wait()
    total = proj[...] + hrecv[...]
    rest = full(wblocks, row) - dot_exact(rowside[:, :width], total, NN)
    rowside[:, width:] = dot_exact(dot_exact(rest, linv, NT), linv, NN)
    pgather.finish()
    wgather.finish()
    pstore.wait()
    wstore.wait()


def update_kernel(trailing, pcols, wcols, rowside, basis, updated, basis_out, high, low):
    @pl.when(pl.program_id(0) == 0)
    def _():
        high[...], low[...] = split(rowside[...])
        basis_out[...] = basis[...]

    values = jnp.concatenate([wcols[0, 0], wcols[1, 0], pcols[0, 0], pcols[1, 0]], 1)
    updated[...] = trailing[...] - dot_split((high[...], low[...]), split(values), NT)


def update(trailing, pcols, wcols, rowside, basis):
    height, width = basis.shape
    _, blocks, _, half = pcols.shape
    square = pl.BlockSpec((height, height), lambda j: (0, j))
    column = pl.BlockSpec((2, 1, height, half), lambda j: (0, j, 0, 0))
    whole = lambda *shape: pl.BlockSpec(shape, lambda j: (0, 0))
    return pl.pallas_call(
        update_kernel,
        grid=(blocks,),
        out_shape=(jax.ShapeDtypeStruct(trailing.shape, jnp.float32),
                   jax.ShapeDtypeStruct(basis.shape, jnp.float32)),
        in_specs=[square, column, column, whole(height, 2 * width), whole(height, width)],
        out_specs=[square, whole(height, width)],
        scratch_shapes=[pltpu.VMEM((height, 2 * width), jnp.bfloat16)] * 2,
        compiler_params=pltpu.CompilerParams(vmem_limit_bytes=40 * 2**20),
        name="update",
    )(trailing, pcols, wcols, rowside, basis)


def fused(trailing, panel, rows):
    height, half = panel.shape
    width = 2 * half
    planes = rows // PLANE
    blocks = (2, rows, height, half)
    dma = pltpu.SemaphoreType.DMA
    vmem = lambda *shape: pltpu.VMEM(shape, jnp.float32)
    gather_sems = [dma((planes,)), dma((planes,)), dma((planes, 2)), dma((rows,)), dma((rows,)),
                   dma((rows,))]
    return pl.pallas_call(
        functools.partial(kernel, planes),
        out_shape=tuple(jax.ShapeDtypeStruct(shape, jnp.float32) for shape in (
            (2, rows // 2, height, half), (2, rows // 2, height, half), (height, 2 * width),
            (height, width))),
        in_specs=[pl.BlockSpec(memory_space=pl.ANY), pl.BlockSpec(memory_space=pltpu.VMEM)],
        out_specs=[pl.BlockSpec(memory_space=pl.ANY)] * 2
        + [pl.BlockSpec(memory_space=pltpu.VMEM)] * 2,
        scratch_shapes=[
            vmem(*trailing.shape), vmem(*blocks), vmem(*blocks), vmem(2, height, half),
            vmem(height, half), vmem(width, width), vmem(width, width), vmem(width, width),
            vmem(width, width), vmem(width, 2 * width), vmem(width, 2 * width),
            dma, dma((2,)), *gather_sems, *gather_sems, dma((3,)), dma((3,)),
        ],
        compiler_params=pltpu.CompilerParams(
            collective_id=0, has_side_effects=True, vmem_limit_bytes=56 * 2**20
        ),
        name="panel_update",
    )(trailing, panel)


def shards(trailing, panel):
    rows, cols = lax.axis_size("prow"), lax.axis_size("pcol")
    if cols == 2 and rows % (2 * PLANE) == 0 and panel.shape[1] % 128 == 0:
        return tuple(update(trailing, *fused(trailing, panel, rows)))
    gather = lambda value: lax.all_to_all(
        lax.all_gather(value, "prow", axis=0, tiled=True), "pcol", 0, 1, tiled=True
    )
    panel_rows = lax.all_gather(panel, "pcol", axis=1, tiled=True)
    panel_cols = gather(panel)
    gram = lax.psum(matmul(panel_cols.T, panel_cols), "pcol")
    factor = jnp.linalg.cholesky(gram)
    solve = functools.partial(
        lax.linalg.triangular_solve, factor, left_side=False, lower=True, transpose_a=True
    )
    basis_rows, basis_cols = solve(panel_rows), solve(panel_cols)
    part = lax.psum_scatter(
        matmul(trailing, basis_cols), "pcol", scatter_dimension=1, tiled=True
    )
    product_rows = lax.all_gather(part, "pcol", axis=1, tiled=True)
    product_cols = gather(part)
    projected = lax.psum(matmul(basis_cols.T, product_cols), "pcol")
    correction = product_rows - 0.5 * matmul(basis_rows, projected)
    correction_cols = product_cols - 0.5 * matmul(basis_cols, projected)
    updated = trailing - matmul(basis_rows, correction_cols.T) - matmul(correction, basis_cols.T)
    return (updated, basis_rows)


def solution(mesh):
    in_specs = (P("prow", "pcol"), P("prow", "pcol"))
    out_specs = (P("prow", "pcol"), P("prow", None))
    return jax.shard_map(shards, mesh=mesh, in_specs=in_specs, out_specs=out_specs, check_vma=False)
```

```python
import functools
import jax
import jax.numpy as jnp
from jax import lax
from jax.experimental import pallas as pl
from jax.experimental.pallas import tpu as pltpu
from jax.sharding import PartitionSpec as P

MESH = pl.DeviceIdType.MESH
SUB = 8
PLANE = 4
BLOCK = 128
CHUNKS = 2


def matmul(left, right):
    return jnp.dot(left, right, precision=lax.Precision.HIGHEST, preferred_element_type=jnp.float32)


def dot_exact(left, right, dims):
    return lax.dot_general(
        left, right, (dims, ((), ())), precision=lax.Precision.HIGHEST,
        preferred_element_type=jnp.float32,
    )


def split(value):
    high = value.astype(jnp.bfloat16)
    low = (value - high.astype(jnp.float32)).astype(jnp.bfloat16)
    return high, low


def dot_split(left, right, dims):
    dot = functools.partial(
        lax.dot_general, dimension_numbers=(dims, ((), ())), preferred_element_type=jnp.float32
    )
    (left_high, left_low), (right_high, right_low) = left, right
    return dot(left_high, right_high) + (dot(left_high, right_low) + dot(left_low, right_high))


NN = ((1,), (0,))
NT = ((1,), (1,))
TN = ((0,), (0,))


def factor_rows(index, lo, work, upper):
    hi = lo + upper.shape[1] // 2 + BLOCK
    start = pl.multiple_of(index * SUB, SUB)
    rows = work[pl.ds(start, SUB), lo:hi]
    lane = lax.broadcasted_iota(jnp.int32, (SUB, BLOCK), 1)
    sub = lax.broadcasted_iota(jnp.int32, (SUB, BLOCK), 0)
    diagonal = [
        jnp.broadcast_to(
            jnp.sum(jnp.where(lane == start - lo + i, rows[:, :BLOCK], 0.0), axis=1, keepdims=True),
            (SUB, BLOCK),
        )
        for i in range(SUB)
    ]
    unit = [jnp.where(sub == i, 1.0, 0.0).astype(jnp.float32) for i in range(SUB)]
    pivots = diagonal[0]
    for i in range(SUB):
        pivots = jnp.where(sub == i, diagonal[i], pivots)
        if i + 1 < SUB:
            pivot = jnp.broadcast_to(diagonal[i][i : i + 1, :], (SUB, BLOCK))
            ratio = jnp.where(sub > i, diagonal[i], 0.0) * pl.reciprocal(pivot)
            for k in range(i + 1, SUB):
                diagonal[k] = diagonal[k] - ratio * diagonal[k][i : i + 1, :]
            for k in range(i + 1):
                unit[k] = unit[k] - ratio * unit[k][i : i + 1, :]
    scale = lax.rsqrt(pivots)
    scale = scale * (1.5 - 0.5 * (pivots * scale) * scale)
    reduced = jnp.zeros_like(rows)
    for i in range(SUB):
        weight = jnp.concatenate([scale * unit[i]] * (rows.shape[1] // BLOCK), 1)
        reduced = reduced + weight * rows[i : i + 1, :]
    upper[pl.ds(start, SUB), lo:hi] = reduced
    high = reduced.astype(jnp.bfloat16).astype(jnp.float32)
    rest = reduced - high
    mid = rest.astype(jnp.bfloat16).astype(jnp.float32)
    low = rest - mid
    left = jnp.concatenate([part[:, :BLOCK] for part in (high, high, mid, high, low, mid)], 0)
    right = jnp.concatenate([high, mid, high, low, high, mid], 0)
    work[lo : lo + BLOCK, lo:hi] -= lax.dot_general(
        left.astype(jnp.bfloat16), right.astype(jnp.bfloat16), (TN, ((), ())),
        preferred_element_type=jnp.float32,
    )


def factor_below(lo, work, upper):
    width = upper.shape[1] // 2
    mid, hi = lo + BLOCK, lo + width + BLOCK
    if mid < width:
        work[mid:, mid:hi] -= dot_exact(upper[lo:mid, mid:width], upper[lo:mid, mid:hi], TN)


def kernel(planes, trailing, panel, pcols, wcols, rowside, basis_out, held, pblocks, wblocks,
           partial, wrecv, gram, grecv, proj, hrecv, work, upper, load_sem, store_sem, pz, p1, p2, ps, precv, psib, wz, w1, w2, ws, wr, wsib,
           swap_send, swap_recv):
    row, col = lax.axis_index("prow"), lax.axis_index("pcol")
    height, half = panel.shape
    width = 2 * half
    depth = row // PLANE
    place = lax.rem(row, PLANE)
    stride1 = 2 - col
    stride2 = 1 + col
    flip1 = stride1 * (1 - 2 * lax.rem(place // stride1, 2))
    flip2 = stride2 * (1 - 2 * lax.rem(place // stride2, 2))
    other = 1 - col
    near = planes // 2
    chunk = height // CHUNKS

    upper_half = depth // near
    mirrored = depth + upper_half * (planes - 1 - 2 * depth)

    def plane_of(k):
        plane = k + (1 - 2 * k) * mirrored if k < 2 else k
        return plane + upper_half * (planes - 1 - 2 * plane)

    load = pltpu.make_async_copy(trailing, held, load_sem)
    load.start()
    barrier = pltpu.get_barrier_semaphore()
    peers = [(plane_of(k) * PLANE + place, col) for k in range(1, planes)]
    peers += [(row + flip1, col), (row + flip2, col), (row, other)]
    for peer in peers:
        pl.semaphore_signal(barrier, inc=1, device_id=peer, device_id_type=MESH)
    pl.semaphore_wait(barrier, len(peers))

    class Gather:
        def __init__(self, blocks, sends, recv, sib):
            self.blocks, self.recv, self.sib = blocks, recv, sib
            self.sz, self.s1, self.s2, self.ss = sends

        def part(self, which, block, h):
            return self.blocks.at[which, block, pl.ds(h * chunk, chunk)]

        def copy(self, which, block, h, sem, recv, to):
            ref = self.part(which, block, h)
            return pltpu.make_async_remote_copy(
                src_ref=ref, dst_ref=ref, send_sem=sem, recv_sem=recv.at[block, h],
                device_id=to, device_id_type=MESH,
            )

        def zcopy(self, k, h):
            return self.copy(col, row, h, self.sz.at[k, h], self.recv,
                             (plane_of(k) * PLANE + place, col))

        def copy1(self, k, h):
            return self.copy(col, plane_of(k) * PLANE + place, h, self.s1.at[k, h], self.recv,
                             (row + flip1, col))

        def copy2(self, k, h, hop):
            return self.copy(col, plane_of(k) * PLANE + place + hop * flip1, h,
                             self.s2.at[k, hop, h], self.recv, (row + flip2, col))

        def copys(self, block, h):
            return self.copy(col, block, h, self.ss.at[block, h], self.sib, (row, other))

        def arrived(self, block, h):
            self.copy(col, block, h, self.sz.at[0, 0], self.recv, (row, other)).wait_recv()

        def sibling_arrived(self, block, h):
            self.copy(other, block, h, self.sz.at[0, 0], self.sib, (row, other)).wait_recv()

        def own_arrived(self):
            for h in range(CHUNKS):
                self.sibling_arrived(row, h)

        def first(self):
            for h in range(CHUNKS):
                self.copy1(0, h).start()
                self.copy2(0, h, 0).start()
                for k in range(1, planes):
                    self.zcopy(k, h).start()
            for h in range(CHUNKS):
                self.copys(row, h).start()

        def forward0(self, k, h):
            self.arrived(plane_of(k) * PLANE + place, h)
            self.copy1(k, h).start()
            self.copy2(k, h, 0).start()

        def forward1(self, k, h):
            self.arrived(plane_of(k) * PLANE + place + flip1, h)
            self.copy2(k, h, 1).start()

        def others(self, k, act):
            for b in range(PLANE):
                block = plane_of(k) * PLANE + b
                if k:
                    act(block)
                else:
                    pl.when(block != row)(functools.partial(act, block))

        def forward2(self, k, h):
            for hop in range(2):
                self.arrived(plane_of(k) * PLANE + place + flip2 + hop * flip1, h)

            @pl.when(plane_of(k) // near != col)
            def _():
                self.others(k, lambda block: self.copys(block, h).start())

        def sibling(self, k):
            for h in range(CHUNKS):
                self.others(k, lambda block: self.sibling_arrived(block, h))

        def steps(self):
            items = [(k, h) for k in range(planes) for h in range(CHUNKS)]
            out = []
            for t in range(len(items) + 2):
                for lag, step in ((0, self.forward0), (1, self.forward1), (2, self.forward2)):
                    if 0 <= t - lag < len(items):
                        k, h = items[t - lag]
                        if lag or k:
                            out.append((step, (k, h)))
            return out

        def finish(self):
            for h in range(CHUNKS):
                self.copys(row, h).wait_send()
                for k in range(planes):
                    if k:
                        self.zcopy(k, h).wait_send()
                    self.copy1(k, h).wait_send()
                    for hop in range(2):
                        self.copy2(k, h, hop).wait_send()

                    @pl.when(plane_of(k) // near != col)
                    def _():
                        self.others(k, lambda block: self.copys(block, h).wait_send())

    def full(blocks, block):
        return jnp.concatenate([blocks[0, block], blocks[1, block]], 1)

    def swap(source, target, slot):
        return pltpu.make_async_remote_copy(
            src_ref=source, dst_ref=target, send_sem=swap_send.at[slot],
            recv_sem=swap_recv.at[slot], device_id=(row, other), device_id_type=MESH,
        )

    pgather = Gather(pblocks, (pz, p1, p2, ps), precv, psib)
    pblocks[col, row] = panel[...]
    pgather.first()
    partial[...] = jnp.zeros_like(partial)
    gram[...] = jnp.zeros_like(gram)
    load.wait()
    pgather.own_arrived()

    def multiply(k):
        @pl.when(plane_of(k) // near == col)
        def _():
            pgather.sibling(k)

            @pl.loop(0, PLANE)
            def _(b):
                block = plane_of(k) * PLANE + b
                columns = pl.ds(pl.multiple_of((block - col * near * PLANE) * height, height), height)
                values = full(pblocks, block)
                product = dot_split(split(held[:, columns]), split(values), NN)
                partial[0] += product[:, :half]
                partial[1] += product[:, half:]
                gram[...] += dot_exact(values, values, TN)

    for step, (k, h) in pgather.steps():
        step(k, h)
        if step == pgather.forward2 and h == CHUNKS - 1:
            multiply(k)

    wswap = swap(partial.at[other], wrecv, 0)
    wswap.start()
    gswap = swap(gram, grecv, 1)
    gswap.start()
    wswap.wait()
    wblocks[col, row] = partial[col] + wrecv[...]
    wgather = Gather(wblocks, (wz, w1, w2, ws), wr, wsib)
    wgather.first()
    gswap.wait()
    work[:, :width] = gram[...] + grecv[...]
    work[:, width:] = jnp.where(
        lax.broadcasted_iota(jnp.int32, (width, width), 0)
        == lax.broadcasted_iota(jnp.int32, (width, width), 1), 1.0, 0.0)

    upper[...] = jnp.zeros_like(upper)
    proj[...] = jnp.zeros_like(proj)
    mine = pl.ds(col * near * PLANE, near * PLANE)
    pstore = pltpu.make_async_copy(pblocks.at[:, mine], pcols, store_sem.at[0])
    pstore.start()

    def project(k):
        @pl.when(plane_of(k) // near == col)
        def _():
            wgather.sibling(k)

            @pl.loop(0, PLANE)
            def _(b):
                block = plane_of(k) * PLANE + b
                proj[...] += dot_exact(full(pblocks, block), full(wblocks, block), TN)

    wsteps = wgather.steps()
    for k in range(planes):
        wsteps.insert(wsteps.index((wgather.forward2, (k, CHUNKS - 1))) + 2, (project, (k,)))
    wsteps.insert(0, (wgather.own_arrived, ()))
    count = BLOCK // SUB
    pieces = 8
    each = -(-len(wsteps) // (pieces * (width // BLOCK)))
    for lo in range(0, width, BLOCK):
        for piece in range(pieces):
            first, last = count * piece // pieces, count * (piece + 1) // pieces
            lax.fori_loop(lo // SUB + first, lo // SUB + last,
                          lambda j, _: (factor_rows(j, lo, work, upper), 0)[1], 0)
            for step, at in wsteps[:each]:
                step(*at)
            wsteps = wsteps[each:]
        factor_below(lo, work, upper)

    linv = upper[:, width:]
    basis = dot_exact(full(pblocks, row), linv, NT)
    basis_out[...] = basis
    rowside[:, :width] = dot_exact(basis, linv, NN)
    for step, at in wsteps:
        step(*at)
    hswap = swap(proj, hrecv, 2)
    hswap.start()
    wstore = pltpu.make_async_copy(wblocks.at[:, mine], wcols, store_sem.at[1])
    wstore.start()
    hswap.wait()
    total = proj[...] + hrecv[...]
    rest = full(wblocks, row) - dot_exact(rowside[:, :width], total, NN)
    rowside[:, width:] = dot_exact(dot_exact(rest, linv, NT), linv, NN)
    pgather.finish()
    wgather.finish()
    pstore.wait()
    wstore.wait()


def update_kernel(trailing, pcols, wcols, rowside, basis, updated, basis_out, left, right):
    depth = rowside.shape[1]

    @pl.when(pl.program_id(0) == 0)
    def _():
        high, low = split(rowside[...])
        left[:, :depth], left[:, depth : 2 * depth], left[:, 2 * depth :] = high, high, low
        basis_out[...] = basis[...]

    for i, ref in enumerate((wcols, pcols)):
        for j in range(2):
            half = ref.shape[3]
            high, low = split(ref[j, 0])
            for part, value in enumerate((high, low, high)):
                start = part * depth + (2 * i + j) * half
                right[:, start : start + half] = value
    updated[...] = trailing[...] - lax.dot_general(
        left[...], right[...], (NT, ((), ())), preferred_element_type=jnp.float32
    )


def update(trailing, pcols, wcols, rowside, basis):
    height, width = basis.shape
    _, blocks, _, half = pcols.shape
    square = pl.BlockSpec((height, height), lambda j: (0, j))
    column = pl.BlockSpec((2, 1, height, half), lambda j: (0, j, 0, 0))
    whole = lambda *shape: pl.BlockSpec(shape, lambda j: (0, 0))
    return pl.pallas_call(
        update_kernel,
        grid=(blocks,),
        out_shape=(jax.ShapeDtypeStruct(trailing.shape, jnp.float32),
                   jax.ShapeDtypeStruct(basis.shape, jnp.float32)),
        in_specs=[square, column, column, whole(height, 2 * width), whole(height, width)],
        out_specs=[square, whole(height, width)],
        scratch_shapes=[pltpu.VMEM((height, 6 * width), jnp.bfloat16)] * 2,
        compiler_params=pltpu.CompilerParams(vmem_limit_bytes=60 * 2**20),
        name="update",
    )(trailing, pcols, wcols, rowside, basis)


def fused(trailing, panel, rows):
    height, half = panel.shape
    width = 2 * half
    planes = rows // PLANE
    blocks = (2, rows, height, half)
    dma = pltpu.SemaphoreType.DMA
    vmem = lambda *shape: pltpu.VMEM(shape, jnp.float32)
    gather_sems = [dma((planes, CHUNKS)), dma((planes, CHUNKS)), dma((planes, 2, CHUNKS)),
                   dma((rows, CHUNKS)), dma((rows, CHUNKS)), dma((rows, CHUNKS))]
    return pl.pallas_call(
        functools.partial(kernel, planes),
        out_shape=tuple(jax.ShapeDtypeStruct(shape, jnp.float32) for shape in (
            (2, rows // 2, height, half), (2, rows // 2, height, half), (height, 2 * width),
            (height, width))),
        in_specs=[pl.BlockSpec(memory_space=pl.ANY), pl.BlockSpec(memory_space=pltpu.VMEM)],
        out_specs=[pl.BlockSpec(memory_space=pl.ANY)] * 2
        + [pl.BlockSpec(memory_space=pltpu.VMEM)] * 2,
        scratch_shapes=[
            vmem(*trailing.shape), vmem(*blocks), vmem(*blocks), vmem(2, height, half),
            vmem(height, half), vmem(width, width), vmem(width, width), vmem(width, width),
            vmem(width, width), vmem(width, 2 * width), vmem(width, 2 * width),
            dma, dma((2,)), *gather_sems, *gather_sems, dma((3,)), dma((3,)),
        ],
        compiler_params=pltpu.CompilerParams(
            collective_id=0, has_side_effects=True, vmem_limit_bytes=56 * 2**20
        ),
        name="panel_update",
    )(trailing, panel)


def shards(trailing, panel):
    rows, cols = lax.axis_size("prow"), lax.axis_size("pcol")
    if cols == 2 and rows == 4 * PLANE and panel.shape[1] % 128 == 0:
        return tuple(update(trailing, *fused(trailing, panel, rows)))
    gather = lambda value: lax.all_to_all(
        lax.all_gather(value, "prow", axis=0, tiled=True), "pcol", 0, 1, tiled=True
    )
    panel_rows = lax.all_gather(panel, "pcol", axis=1, tiled=True)
    panel_cols = gather(panel)
    gram = lax.psum(matmul(panel_cols.T, panel_cols), "pcol")
    factor = jnp.linalg.cholesky(gram)
    solve = functools.partial(
        lax.linalg.triangular_solve, factor, left_side=False, lower=True, transpose_a=True
    )
    basis_rows, basis_cols = solve(panel_rows), solve(panel_cols)
    part = lax.psum_scatter(
        matmul(trailing, basis_cols), "pcol", scatter_dimension=1, tiled=True
    )
    product_rows = lax.all_gather(part, "pcol", axis=1, tiled=True)
    product_cols = gather(part)
    projected = lax.psum(matmul(basis_cols.T, product_cols), "pcol")
    correction = product_rows - 0.5 * matmul(basis_rows, projected)
    correction_cols = product_cols - 0.5 * matmul(basis_cols, projected)
    updated = trailing - matmul(basis_rows, correction_cols.T) - matmul(correction, basis_cols.T)
    return (updated, basis_rows)


def solution(mesh):
    in_specs = (P("prow", "pcol"), P("prow", "pcol"))
    out_specs = (P("prow", "pcol"), P("prow", None))
    return jax.shard_map(shards, mesh=mesh, in_specs=in_specs, out_specs=out_specs, check_vma=False)
```

```python
import functools
import jax
import jax.numpy as jnp
from jax import lax
from jax.experimental import pallas as pl
from jax.experimental.pallas import tpu as pltpu
from jax.sharding import PartitionSpec as P

MESH = pl.DeviceIdType.MESH
SUB = 8
PLANE = 4
BLOCK = 128
CHUNKS = 2


def matmul(left, right):
    return jnp.dot(left, right, precision=lax.Precision.HIGHEST, preferred_element_type=jnp.float32)


def dot_exact(left, right, dims):
    return lax.dot_general(
        left, right, (dims, ((), ())), precision=lax.Precision.HIGHEST,
        preferred_element_type=jnp.float32,
    )


def split(value):
    high = value.astype(jnp.bfloat16)
    low = (value - high.astype(jnp.float32)).astype(jnp.bfloat16)
    return high, low


def dot_split(left, right, dims):
    dot = functools.partial(
        lax.dot_general, dimension_numbers=(dims, ((), ())), preferred_element_type=jnp.float32
    )
    (left_high, left_low), (right_high, right_low) = left, right
    return dot(left_high, right_high) + (dot(left_high, right_low) + dot(left_low, right_high))


NN = ((1,), (0,))
NT = ((1,), (1,))
TN = ((0,), (0,))


def factor_rows(index, lo, work, upper):
    hi = lo + upper.shape[1] // 2 + BLOCK
    start = pl.multiple_of(index * SUB, SUB)
    rows = work[pl.ds(start, SUB), lo:hi]
    lane = lax.broadcasted_iota(jnp.int32, (SUB, BLOCK), 1)
    sub = lax.broadcasted_iota(jnp.int32, (SUB, BLOCK), 0)
    diagonal = [
        jnp.broadcast_to(
            jnp.sum(jnp.where(lane == start - lo + i, rows[:, :BLOCK], 0.0), axis=1, keepdims=True),
            (SUB, BLOCK),
        )
        for i in range(SUB)
    ]
    unit = [jnp.where(sub == i, 1.0, 0.0).astype(jnp.float32) for i in range(SUB)]
    pivots = diagonal[0]
    for i in range(SUB):
        pivots = jnp.where(sub == i, diagonal[i], pivots)
        if i + 1 < SUB:
            pivot = jnp.broadcast_to(diagonal[i][i : i + 1, :], (SUB, BLOCK))
            ratio = jnp.where(sub > i, diagonal[i], 0.0) * pl.reciprocal(pivot)
            for k in range(i + 1, SUB):
                diagonal[k] = diagonal[k] - ratio * diagonal[k][i : i + 1, :]
            for k in range(i + 1):
                unit[k] = unit[k] - ratio * unit[k][i : i + 1, :]
    scale = lax.rsqrt(pivots)
    scale = scale * (1.5 - 0.5 * (pivots * scale) * scale)
    reduced = jnp.zeros_like(rows)
    for i in range(SUB):
        weight = jnp.concatenate([scale * unit[i]] * (rows.shape[1] // BLOCK), 1)
        reduced = reduced + weight * rows[i : i + 1, :]
    upper[pl.ds(start, SUB), lo:hi] = reduced
    high = reduced.astype(jnp.bfloat16).astype(jnp.float32)
    rest = reduced - high
    mid = rest.astype(jnp.bfloat16).astype(jnp.float32)
    low = rest - mid
    left = jnp.concatenate([part[:, :BLOCK] for part in (high, high, mid, high, low, mid)], 0)
    right = jnp.concatenate([high, mid, high, low, high, mid], 0)
    work[lo : lo + BLOCK, lo:hi] -= lax.dot_general(
        left.astype(jnp.bfloat16), right.astype(jnp.bfloat16), (TN, ((), ())),
        preferred_element_type=jnp.float32,
    )


def factor_below(lo, work, upper):
    width = upper.shape[1] // 2
    mid, hi = lo + BLOCK, lo + width + BLOCK
    if mid < width:
        work[mid:, mid:hi] -= dot_exact(upper[lo:mid, mid:width], upper[lo:mid, mid:hi], TN)


def kernel(planes, trailing, panel, pcols, wcols, rowside, basis_out, held, pblocks, wblocks,
           partial, wrecv, gram, grecv, proj, hrecv, work, upper, load_sem, store_sem, pz, p1, p2, ps, precv, psib, wz, w1, w2, ws, wr, wsib,
           swap_send, swap_recv):
    row, col = lax.axis_index("prow"), lax.axis_index("pcol")
    height, half = panel.shape
    width = 2 * half
    depth = row // PLANE
    place = lax.rem(row, PLANE)
    stride1 = 2 - col
    stride2 = 1 + col
    flip1 = stride1 * (1 - 2 * lax.rem(place // stride1, 2))
    flip2 = stride2 * (1 - 2 * lax.rem(place // stride2, 2))
    other = 1 - col
    near = planes // 2
    chunk = height // CHUNKS

    upper_half = depth // near
    mirrored = depth + upper_half * (planes - 1 - 2 * depth)

    def plane_of(k):
        plane = k + (1 - 2 * k) * mirrored if k < 2 else k
        return plane + upper_half * (planes - 1 - 2 * plane)

    load = pltpu.make_async_copy(trailing, held, load_sem)
    load.start()
    barrier = pltpu.get_barrier_semaphore()
    peers = [(plane_of(k) * PLANE + place, col) for k in range(1, planes)]
    peers += [(row + flip1, col), (row + flip2, col), (row, other)]
    for peer in peers:
        pl.semaphore_signal(barrier, inc=1, device_id=peer, device_id_type=MESH)
    pl.semaphore_wait(barrier, len(peers))

    class Gather:
        def __init__(self, blocks, sends, recv, sib):
            self.blocks, self.recv, self.sib = blocks, recv, sib
            self.sz, self.s1, self.s2, self.ss = sends

        def part(self, which, block, h):
            return self.blocks.at[which, block, pl.ds(h * chunk, chunk)]

        def copy(self, which, block, h, sem, recv, to):
            ref = self.part(which, block, h)
            return pltpu.make_async_remote_copy(
                src_ref=ref, dst_ref=ref, send_sem=sem, recv_sem=recv.at[block, h],
                device_id=to, device_id_type=MESH,
            )

        def zcopy(self, k, h):
            return self.copy(col, row, h, self.sz.at[k, h], self.recv,
                             (plane_of(k) * PLANE + place, col))

        def copy1(self, k, h):
            return self.copy(col, plane_of(k) * PLANE + place, h, self.s1.at[k, h], self.recv,
                             (row + flip1, col))

        def copy2(self, k, h, hop):
            return self.copy(col, plane_of(k) * PLANE + place + hop * flip1, h,
                             self.s2.at[k, hop, h], self.recv, (row + flip2, col))

        def copys(self, block, h):
            return self.copy(col, block, h, self.ss.at[block, h], self.sib, (row, other))

        def arrived(self, block, h):
            self.copy(col, block, h, self.sz.at[0, 0], self.recv, (row, other)).wait_recv()

        def sibling_arrived(self, block, h):
            self.copy(other, block, h, self.sz.at[0, 0], self.sib, (row, other)).wait_recv()

        def own_arrived(self):
            for h in range(CHUNKS):
                self.sibling_arrived(row, h)

        def first(self):
            for h in range(CHUNKS):
                self.copy1(0, h).start()
                self.copy2(0, h, 0).start()
                for k in range(1, planes):
                    self.zcopy(k, h).start()
            for h in range(CHUNKS):
                self.copys(row, h).start()

        def offset(self, k, i):
            return plane_of(k) * PLANE + place + lax.rem(i, 2) * flip1 + i // 2 * flip2

        def hand_over(self, k, h, i):
            @pl.when(plane_of(k) // near != col)
            def _():
                self.copys(self.offset(k, i), h).start()

        def forward0(self, k, h):
            self.arrived(self.offset(k, 0), h)
            self.copy1(k, h).start()
            self.copy2(k, h, 0).start()
            self.hand_over(k, h, 0)

        def forward1(self, k, h):
            self.arrived(self.offset(k, 1), h)
            self.copy2(k, h, 1).start()
            self.hand_over(k, h, 1)

        def forward2(self, k, h):
            for i in (2, 3):
                self.arrived(self.offset(k, i), h)
                self.hand_over(k, h, i)

        def steps(self, use):
            def pair(k, g):
                @pl.when(plane_of(k) // near == col)
                def _():
                    for i in (2 * g, 2 * g + 1):
                        for h in range(CHUNKS):
                            if k or i:
                                self.sibling_arrived(self.offset(k, i), h)

                    @pl.loop(2 * g, 2 * g + 2)
                    def _(i):
                        use(self.offset(k, i))

            items = [(k, h) for k in range(planes) for h in range(CHUNKS)]
            out, ready, waiting = [(self.own_arrived, ())], [], []
            for t in range(len(items) + 2):
                ready, waiting = ready + waiting, []
                for lag, step in ((0, self.forward0), (1, self.forward1), (2, self.forward2)):
                    if 0 <= t - lag < len(items):
                        k, h = items[t - lag]
                        if lag or k:
                            out.append((step, (k, h)))
                        if lag and h == CHUNKS - 1:
                            waiting.append((pair, (k, lag - 1)))
                out += ready[:1]
                ready = ready[1:]
            return out + ready + waiting

        def finish(self):
            for h in range(CHUNKS):
                self.copys(row, h).wait_send()
                for k in range(planes):
                    if k:
                        self.zcopy(k, h).wait_send()
                    self.copy1(k, h).wait_send()
                    for hop in range(2):
                        self.copy2(k, h, hop).wait_send()

                    @pl.when(plane_of(k) // near != col)
                    def _():
                        for i in range(PLANE):
                            if k or i:
                                self.copys(self.offset(k, i), h).wait_send()

    def full(blocks, block):
        return jnp.concatenate([blocks[0, block], blocks[1, block]], 1)

    def swap(source, target, slot):
        return pltpu.make_async_remote_copy(
            src_ref=source, dst_ref=target, send_sem=swap_send.at[slot],
            recv_sem=swap_recv.at[slot], device_id=(row, other), device_id_type=MESH,
        )

    pgather = Gather(pblocks, (pz, p1, p2, ps), precv, psib)
    pblocks[col, row] = panel[...]
    pgather.first()
    partial[...] = jnp.zeros_like(partial)
    gram[...] = jnp.zeros_like(gram)
    load.wait()

    def multiply(block):
        columns = pl.ds(pl.multiple_of((block - col * near * PLANE) * height, height), height)
        values = full(pblocks, block)
        product = dot_split(split(held[:, columns]), split(values), NN)
        partial[0] += product[:, :half]
        partial[1] += product[:, half:]
        gram[...] += dot_exact(values, values, TN)

    for step, at in pgather.steps(multiply):
        step(*at)

    wswap = swap(partial.at[other], wrecv, 0)
    wswap.start()
    gswap = swap(gram, grecv, 1)
    gswap.start()
    wswap.wait()
    wblocks[col, row] = partial[col] + wrecv[...]
    wgather = Gather(wblocks, (wz, w1, w2, ws), wr, wsib)
    wgather.first()
    gswap.wait()
    work[:, :width] = gram[...] + grecv[...]
    work[:, width:] = jnp.where(
        lax.broadcasted_iota(jnp.int32, (width, width), 0)
        == lax.broadcasted_iota(jnp.int32, (width, width), 1), 1.0, 0.0)

    upper[...] = jnp.zeros_like(upper)
    proj[...] = jnp.zeros_like(proj)
    mine = pl.ds(col * near * PLANE, near * PLANE)
    pstore = pltpu.make_async_copy(pblocks.at[:, mine], pcols, store_sem.at[0])
    pstore.start()

    def project(block):
        proj[...] += dot_exact(full(pblocks, block), full(wblocks, block), TN)

    wsteps = wgather.steps(project)
    count = BLOCK // SUB
    pieces = 8
    each = -(-len(wsteps) // (pieces * (width // BLOCK)))
    for lo in range(0, width, BLOCK):
        for piece in range(pieces):
            first, last = count * piece // pieces, count * (piece + 1) // pieces
            lax.fori_loop(lo // SUB + first, lo // SUB + last,
                          lambda j, _: (factor_rows(j, lo, work, upper), 0)[1], 0)
            for step, at in wsteps[:each]:
                step(*at)
            wsteps = wsteps[each:]
        factor_below(lo, work, upper)

    linv = upper[:, width:]
    basis = dot_exact(full(pblocks, row), linv, NT)
    basis_out[...] = basis
    rowside[:, :width] = dot_exact(basis, linv, NN)
    for step, at in wsteps:
        step(*at)
    hswap = swap(proj, hrecv, 2)
    hswap.start()
    wstore = pltpu.make_async_copy(wblocks.at[:, mine], wcols, store_sem.at[1])
    wstore.start()
    hswap.wait()
    total = proj[...] + hrecv[...]
    rest = full(wblocks, row) - dot_exact(rowside[:, :width], total, NN)
    rowside[:, width:] = dot_exact(dot_exact(rest, linv, NT), linv, NN)
    pgather.finish()
    wgather.finish()
    pstore.wait()
    wstore.wait()


def update_kernel(trailing, pcols, wcols, rowside, basis, updated, basis_out, left, right):
    depth = rowside.shape[1]

    @pl.when(pl.program_id(0) == 0)
    def _():
        high, low = split(rowside[...])
        left[:, :depth], left[:, depth : 2 * depth], left[:, 2 * depth :] = high, high, low
        basis_out[...] = basis[...]

    for i, ref in enumerate((wcols, pcols)):
        for j in range(2):
            half = ref.shape[3]
            high, low = split(ref[j, 0])
            for part, value in enumerate((high, low, high)):
                start = part * depth + (2 * i + j) * half
                right[:, start : start + half] = value
    updated[...] = trailing[...] - lax.dot_general(
        left[...], right[...], (NT, ((), ())), preferred_element_type=jnp.float32
    )


def update(trailing, pcols, wcols, rowside, basis):
    height, width = basis.shape
    _, blocks, _, half = pcols.shape
    square = pl.BlockSpec((height, height), lambda j: (0, j))
    column = pl.BlockSpec((2, 1, height, half), lambda j: (0, j, 0, 0))
    whole = lambda *shape: pl.BlockSpec(shape, lambda j: (0, 0))
    return pl.pallas_call(
        update_kernel,
        grid=(blocks,),
        out_shape=(jax.ShapeDtypeStruct(trailing.shape, jnp.float32),
                   jax.ShapeDtypeStruct(basis.shape, jnp.float32)),
        in_specs=[square, column, column, whole(height, 2 * width), whole(height, width)],
        out_specs=[square, whole(height, width)],
        scratch_shapes=[pltpu.VMEM((height, 6 * width), jnp.bfloat16)] * 2,
        compiler_params=pltpu.CompilerParams(vmem_limit_bytes=60 * 2**20),
        name="update",
    )(trailing, pcols, wcols, rowside, basis)


def fused(trailing, panel, rows):
    height, half = panel.shape
    width = 2 * half
    planes = rows // PLANE
    blocks = (2, rows, height, half)
    dma = pltpu.SemaphoreType.DMA
    vmem = lambda *shape: pltpu.VMEM(shape, jnp.float32)
    gather_sems = [dma((planes, CHUNKS)), dma((planes, CHUNKS)), dma((planes, 2, CHUNKS)),
                   dma((rows, CHUNKS)), dma((rows, CHUNKS)), dma((rows, CHUNKS))]
    return pl.pallas_call(
        functools.partial(kernel, planes),
        out_shape=tuple(jax.ShapeDtypeStruct(shape, jnp.float32) for shape in (
            (2, rows // 2, height, half), (2, rows // 2, height, half), (height, 2 * width),
            (height, width))),
        in_specs=[pl.BlockSpec(memory_space=pl.ANY), pl.BlockSpec(memory_space=pltpu.VMEM)],
        out_specs=[pl.BlockSpec(memory_space=pl.ANY)] * 2
        + [pl.BlockSpec(memory_space=pltpu.VMEM)] * 2,
        scratch_shapes=[
            vmem(*trailing.shape), vmem(*blocks), vmem(*blocks), vmem(2, height, half),
            vmem(height, half), vmem(width, width), vmem(width, width), vmem(width, width),
            vmem(width, width), vmem(width, 2 * width), vmem(width, 2 * width),
            dma, dma((2,)), *gather_sems, *gather_sems, dma((3,)), dma((3,)),
        ],
        compiler_params=pltpu.CompilerParams(
            collective_id=0, has_side_effects=True, vmem_limit_bytes=56 * 2**20
        ),
        name="panel_update",
    )(trailing, panel)


def shards(trailing, panel):
    rows, cols = lax.axis_size("prow"), lax.axis_size("pcol")
    if cols == 2 and rows == 4 * PLANE and panel.shape[1] % 128 == 0:
        return tuple(update(trailing, *fused(trailing, panel, rows)))
    gather = lambda value: lax.all_to_all(
        lax.all_gather(value, "prow", axis=0, tiled=True), "pcol", 0, 1, tiled=True
    )
    panel_rows = lax.all_gather(panel, "pcol", axis=1, tiled=True)
    panel_cols = gather(panel)
    gram = lax.psum(matmul(panel_cols.T, panel_cols), "pcol")
    factor = jnp.linalg.cholesky(gram)
    solve = functools.partial(
        lax.linalg.triangular_solve, factor, left_side=False, lower=True, transpose_a=True
    )
    basis_rows, basis_cols = solve(panel_rows), solve(panel_cols)
    part = lax.psum_scatter(
        matmul(trailing, basis_cols), "pcol", scatter_dimension=1, tiled=True
    )
    product_rows = lax.all_gather(part, "pcol", axis=1, tiled=True)
    product_cols = gather(part)
    projected = lax.psum(matmul(basis_cols.T, product_cols), "pcol")
    correction = product_rows - 0.5 * matmul(basis_rows, projected)
    correction_cols = product_cols - 0.5 * matmul(basis_cols, projected)
    updated = trailing - matmul(basis_rows, correction_cols.T) - matmul(correction, basis_cols.T)
    return (updated, basis_rows)


def solution(mesh):
    in_specs = (P("prow", "pcol"), P("prow", "pcol"))
    out_specs = (P("prow", "pcol"), P("prow", None))
    return jax.shard_map(shards, mesh=mesh, in_specs=in_specs, out_specs=out_specs, check_vma=False)
```

```python
import functools
import jax
import jax.numpy as jnp
from jax import lax
from jax.experimental import pallas as pl
from jax.experimental.pallas import tpu as pltpu
from jax.sharding import PartitionSpec as P

MESH = pl.DeviceIdType.MESH
SUB = 8
PLANE = 4
BLOCK = 128
CHUNKS = 4


def matmul(left, right):
    return jnp.dot(left, right, precision=lax.Precision.HIGHEST, preferred_element_type=jnp.float32)


def dot_exact(left, right, dims):
    return lax.dot_general(
        left, right, (dims, ((), ())), precision=lax.Precision.HIGHEST,
        preferred_element_type=jnp.float32,
    )


def split(value):
    high = value.astype(jnp.bfloat16)
    low = (value - high.astype(jnp.float32)).astype(jnp.bfloat16)
    return high, low


def dot_split(left, right, dims):
    dot = functools.partial(
        lax.dot_general, dimension_numbers=(dims, ((), ())), preferred_element_type=jnp.float32
    )
    (left_high, left_low), (right_high, right_low) = left, right
    return dot(left_high, right_high) + (dot(left_high, right_low) + dot(left_low, right_high))


NN = ((1,), (0,))
NT = ((1,), (1,))
TN = ((0,), (0,))


def factor_rows(index, lo, work, upper):
    hi = lo + upper.shape[1] // 2 + BLOCK
    start = pl.multiple_of(index * SUB, SUB)
    rows = work[pl.ds(start, SUB), lo:hi]
    lane = lax.broadcasted_iota(jnp.int32, (SUB, BLOCK), 1)
    sub = lax.broadcasted_iota(jnp.int32, (SUB, BLOCK), 0)
    diagonal = [
        jnp.broadcast_to(
            jnp.sum(jnp.where(lane == start - lo + i, rows[:, :BLOCK], 0.0), axis=1, keepdims=True),
            (SUB, BLOCK),
        )
        for i in range(SUB)
    ]
    unit = [jnp.where(sub == i, 1.0, 0.0).astype(jnp.float32) for i in range(SUB)]
    pivots = diagonal[0]
    for i in range(SUB):
        pivots = jnp.where(sub == i, diagonal[i], pivots)
        if i + 1 < SUB:
            pivot = jnp.broadcast_to(diagonal[i][i : i + 1, :], (SUB, BLOCK))
            ratio = jnp.where(sub > i, diagonal[i], 0.0) * pl.reciprocal(pivot)
            for k in range(i + 1, SUB):
                diagonal[k] = diagonal[k] - ratio * diagonal[k][i : i + 1, :]
            for k in range(i + 1):
                unit[k] = unit[k] - ratio * unit[k][i : i + 1, :]
    scale = lax.rsqrt(pivots)
    scale = scale * (1.5 - 0.5 * (pivots * scale) * scale)
    reduced = jnp.zeros_like(rows)
    for i in range(SUB):
        weight = jnp.concatenate([scale * unit[i]] * (rows.shape[1] // BLOCK), 1)
        reduced = reduced + weight * rows[i : i + 1, :]
    upper[pl.ds(start, SUB), lo:hi] = reduced
    high = reduced.astype(jnp.bfloat16).astype(jnp.float32)
    rest = reduced - high
    mid = rest.astype(jnp.bfloat16).astype(jnp.float32)
    low = rest - mid
    left = jnp.concatenate([part[:, :BLOCK] for part in (high, high, mid, high, low, mid)], 0)
    right = jnp.concatenate([high, mid, high, low, high, mid], 0)
    work[lo : lo + BLOCK, lo:hi] -= lax.dot_general(
        left.astype(jnp.bfloat16), right.astype(jnp.bfloat16), (TN, ((), ())),
        preferred_element_type=jnp.float32,
    )


def factor_below(lo, work, upper):
    width = upper.shape[1] // 2
    mid, hi = lo + BLOCK, lo + width + BLOCK
    if mid < width:
        work[mid:, mid:hi] -= dot_exact(upper[lo:mid, mid:width], upper[lo:mid, mid:hi], TN)


def kernel(planes, trailing, panel, pcols, wcols, rowside, basis_out, held, pblocks, wblocks,
           partial, wrecv, gram, grecv, proj, hrecv, work, upper, load_sem, store_sem, pz, p1, p2, ps, precv, psib, wz, w1, w2, ws, wr, wsib,
           swap_send, swap_recv):
    row, col = lax.axis_index("prow"), lax.axis_index("pcol")
    height, half = panel.shape
    width = 2 * half
    depth = row // PLANE
    place = lax.rem(row, PLANE)
    stride1 = 2 - col
    stride2 = 1 + col
    flip1 = stride1 * (1 - 2 * lax.rem(place // stride1, 2))
    flip2 = stride2 * (1 - 2 * lax.rem(place // stride2, 2))
    other = 1 - col
    near = planes // 2
    chunk = height // CHUNKS

    upper_half = depth // near
    mirrored = depth + upper_half * (planes - 1 - 2 * depth)

    def plane_of(k):
        plane = k + (1 - 2 * k) * mirrored if k < 2 else k
        return plane + upper_half * (planes - 1 - 2 * plane)

    load = pltpu.make_async_copy(trailing, held, load_sem)
    load.start()
    barrier = pltpu.get_barrier_semaphore()
    peers = [(plane_of(k) * PLANE + place, col) for k in range(1, planes)]
    peers += [(row + flip1, col), (row + flip2, col), (row, other)]
    for peer in peers:
        pl.semaphore_signal(barrier, inc=1, device_id=peer, device_id_type=MESH)
    pl.semaphore_wait(barrier, len(peers))

    class Gather:
        def __init__(self, blocks, sends, recv, sib):
            self.blocks, self.recv, self.sib = blocks, recv, sib
            self.sz, self.s1, self.s2, self.ss = sends

        def part(self, which, block, h):
            return self.blocks.at[which, block, pl.ds(h * chunk, chunk)]

        def copy(self, which, block, h, sem, recv, to):
            ref = self.part(which, block, h)
            return pltpu.make_async_remote_copy(
                src_ref=ref, dst_ref=ref, send_sem=sem, recv_sem=recv.at[block, h],
                device_id=to, device_id_type=MESH,
            )

        def zcopy(self, k, h):
            return self.copy(col, row, h, self.sz.at[k, h], self.recv,
                             (plane_of(k) * PLANE + place, col))

        def copy1(self, k, h):
            return self.copy(col, plane_of(k) * PLANE + place, h, self.s1.at[k, h], self.recv,
                             (row + flip1, col))

        def copy2(self, k, h, hop):
            return self.copy(col, plane_of(k) * PLANE + place + hop * flip1, h,
                             self.s2.at[k, hop, h], self.recv, (row + flip2, col))

        def copys(self, block, h):
            return self.copy(col, block, h, self.ss.at[block, h], self.sib, (row, other))

        def arrived(self, block, h):
            self.copy(col, block, h, self.sz.at[0, 0], self.recv, (row, other)).wait_recv()

        def sibling_arrived(self, block, h):
            self.copy(other, block, h, self.sz.at[0, 0], self.sib, (row, other)).wait_recv()

        def own_arrived(self):
            for h in range(CHUNKS):
                self.sibling_arrived(row, h)

        def first(self):
            for h in range(CHUNKS):
                self.copy1(0, h).start()
                self.copy2(0, h, 0).start()
                for k in range(1, planes):
                    self.zcopy(k, h).start()
            for h in range(CHUNKS):
                self.copys(row, h).start()

        def offset(self, k, i):
            return plane_of(k) * PLANE + place + lax.rem(i, 2) * flip1 + i // 2 * flip2

        def hand_over(self, k, h, i):
            @pl.when(plane_of(k) // near != col)
            def _():
                self.copys(self.offset(k, i), h).start()

        def forward0(self, k, h):
            self.arrived(self.offset(k, 0), h)
            self.copy1(k, h).start()
            self.copy2(k, h, 0).start()
            self.hand_over(k, h, 0)

        def forward1(self, k, h):
            self.arrived(self.offset(k, 1), h)
            self.copy2(k, h, 1).start()
            self.hand_over(k, h, 1)

        def forward2(self, k, h):
            for i in (2, 3):
                self.arrived(self.offset(k, i), h)
                self.hand_over(k, h, i)

        def steps(self, use):
            def pair(k, g):
                @pl.when(plane_of(k) // near == col)
                def _():
                    for i in (2 * g, 2 * g + 1):
                        for h in range(CHUNKS):
                            if k or i:
                                self.sibling_arrived(self.offset(k, i), h)

                    @pl.loop(2 * g, 2 * g + 2)
                    def _(i):
                        use(self.offset(k, i))

            items = [(k, h) for k in range(planes) for h in range(CHUNKS)]
            out, ready, waiting = [(self.own_arrived, ())], [], []
            for t in range(len(items) + 2):
                ready, waiting = ready + waiting, []
                for lag, step in ((0, self.forward0), (1, self.forward1), (2, self.forward2)):
                    if 0 <= t - lag < len(items):
                        k, h = items[t - lag]
                        if lag or k:
                            out.append((step, (k, h)))
                        if lag and h == CHUNKS - 1:
                            waiting.append((pair, (k, lag - 1)))
                out += ready[:1]
                ready = ready[1:]
            return out + ready + waiting

        def finish(self):
            for h in range(CHUNKS):
                self.copys(row, h).wait_send()
                for k in range(planes):
                    if k:
                        self.zcopy(k, h).wait_send()
                    self.copy1(k, h).wait_send()
                    for hop in range(2):
                        self.copy2(k, h, hop).wait_send()

                    @pl.when(plane_of(k) // near != col)
                    def _():
                        for i in range(PLANE):
                            if k or i:
                                self.copys(self.offset(k, i), h).wait_send()

    def full(blocks, block):
        return jnp.concatenate([blocks[0, block], blocks[1, block]], 1)

    def swap(source, target, slot):
        return pltpu.make_async_remote_copy(
            src_ref=source, dst_ref=target, send_sem=swap_send.at[slot],
            recv_sem=swap_recv.at[slot], device_id=(row, other), device_id_type=MESH,
        )

    pgather = Gather(pblocks, (pz, p1, p2, ps), precv, psib)
    pblocks[col, row] = panel[...]
    pgather.first()
    partial[...] = jnp.zeros_like(partial)
    gram[...] = jnp.zeros_like(gram)
    load.wait()

    def multiply(block):
        columns = pl.ds(pl.multiple_of((block - col * near * PLANE) * height, height), height)
        values = full(pblocks, block)
        product = dot_split(split(held[:, columns]), split(values), NN)
        partial[0] += product[:, :half]
        partial[1] += product[:, half:]
        gram[...] += dot_exact(values, values, TN)

    for step, at in pgather.steps(multiply):
        step(*at)

    wswap = swap(partial.at[other], wrecv, 0)
    wswap.start()
    gswap = swap(gram, grecv, 1)
    gswap.start()
    wswap.wait()
    wblocks[col, row] = partial[col] + wrecv[...]
    wgather = Gather(wblocks, (wz, w1, w2, ws), wr, wsib)
    wgather.first()
    gswap.wait()
    work[:, :width] = gram[...] + grecv[...]
    work[:, width:] = jnp.where(
        lax.broadcasted_iota(jnp.int32, (width, width), 0)
        == lax.broadcasted_iota(jnp.int32, (width, width), 1), 1.0, 0.0)

    upper[...] = jnp.zeros_like(upper)
    proj[...] = jnp.zeros_like(proj)
    mine = pl.ds(col * near * PLANE, near * PLANE)
    pstore = pltpu.make_async_copy(pblocks.at[:, mine], pcols, store_sem.at[0])
    pstore.start()

    def project(block):
        proj[...] += dot_exact(full(pblocks, block), full(wblocks, block), TN)

    wsteps = wgather.steps(project)
    count = BLOCK // SUB
    pieces = 8
    each = -(-len(wsteps) // (pieces * (width // BLOCK)))
    for lo in range(0, width, BLOCK):
        for piece in range(pieces):
            first, last = count * piece // pieces, count * (piece + 1) // pieces
            lax.fori_loop(lo // SUB + first, lo // SUB + last,
                          lambda j, _: (factor_rows(j, lo, work, upper), 0)[1], 0)
            for step, at in wsteps[:each]:
                step(*at)
            wsteps = wsteps[each:]
        factor_below(lo, work, upper)

    linv = upper[:, width:]
    basis = dot_exact(full(pblocks, row), linv, NT)
    basis_out[...] = basis
    rowside[:, :width] = dot_exact(basis, linv, NN)
    solved = dot_exact(dot_exact(full(wblocks, row), linv, NT), linv, NN)
    work[:, :width] = dot_exact(linv, linv, TN)
    for step, at in wsteps:
        step(*at)
    hswap = swap(proj, hrecv, 2)
    hswap.start()
    wstore = pltpu.make_async_copy(wblocks.at[:, mine], wcols, store_sem.at[1])
    wstore.start()
    hswap.wait()
    total = proj[...] + hrecv[...]
    rowside[:, width:] = solved - dot_exact(
        rowside[:, :width], dot_exact(total, work[:, :width], NN), NN
    )
    pgather.finish()
    wgather.finish()
    pstore.wait()
    wstore.wait()


def update_kernel(trailing, pcols, wcols, rowside, basis, updated, basis_out, left, right):
    depth = rowside.shape[1]

    @pl.when(pl.program_id(0) == 0)
    def _():
        high, low = split(rowside[...])
        left[:, :depth], left[:, depth : 2 * depth], left[:, 2 * depth :] = high, high, low
        basis_out[...] = basis[...]

    for i, ref in enumerate((wcols, pcols)):
        for j in range(2):
            half = ref.shape[3]
            high, low = split(ref[j, 0])
            for part, value in enumerate((high, low, high)):
                start = part * depth + (2 * i + j) * half
                right[:, start : start + half] = value
    updated[...] = trailing[...] - lax.dot_general(
        left[...], right[...], (NT, ((), ())), preferred_element_type=jnp.float32
    )


def update(trailing, pcols, wcols, rowside, basis):
    height, width = basis.shape
    _, blocks, _, half = pcols.shape
    square = pl.BlockSpec((height, height), lambda j: (0, j))
    column = pl.BlockSpec((2, 1, height, half), lambda j: (0, j, 0, 0))
    whole = lambda *shape: pl.BlockSpec(shape, lambda j: (0, 0))
    return pl.pallas_call(
        update_kernel,
        grid=(blocks,),
        out_shape=(jax.ShapeDtypeStruct(trailing.shape, jnp.float32),
                   jax.ShapeDtypeStruct(basis.shape, jnp.float32)),
        in_specs=[square, column, column, whole(height, 2 * width), whole(height, width)],
        out_specs=[square, whole(height, width)],
        scratch_shapes=[pltpu.VMEM((height, 6 * width), jnp.bfloat16)] * 2,
        compiler_params=pltpu.CompilerParams(vmem_limit_bytes=60 * 2**20),
        name="update",
    )(trailing, pcols, wcols, rowside, basis)


def fused(trailing, panel, rows):
    height, half = panel.shape
    width = 2 * half
    planes = rows // PLANE
    blocks = (2, rows, height, half)
    dma = pltpu.SemaphoreType.DMA
    vmem = lambda *shape: pltpu.VMEM(shape, jnp.float32)
    gather_sems = [dma((planes, CHUNKS)), dma((planes, CHUNKS)), dma((planes, 2, CHUNKS)),
                   dma((rows, CHUNKS)), dma((rows, CHUNKS)), dma((rows, CHUNKS))]
    return pl.pallas_call(
        functools.partial(kernel, planes),
        out_shape=tuple(jax.ShapeDtypeStruct(shape, jnp.float32) for shape in (
            (2, rows // 2, height, half), (2, rows // 2, height, half), (height, 2 * width),
            (height, width))),
        in_specs=[pl.BlockSpec(memory_space=pl.ANY), pl.BlockSpec(memory_space=pltpu.VMEM)],
        out_specs=[pl.BlockSpec(memory_space=pl.ANY)] * 2
        + [pl.BlockSpec(memory_space=pltpu.VMEM)] * 2,
        scratch_shapes=[
            vmem(*trailing.shape), vmem(*blocks), vmem(*blocks), vmem(2, height, half),
            vmem(height, half), vmem(width, width), vmem(width, width), vmem(width, width),
            vmem(width, width), vmem(width, 2 * width), vmem(width, 2 * width),
            dma, dma((2,)), *gather_sems, *gather_sems, dma((3,)), dma((3,)),
        ],
        compiler_params=pltpu.CompilerParams(
            collective_id=0, has_side_effects=True, vmem_limit_bytes=56 * 2**20
        ),
        name="panel_update",
    )(trailing, panel)


def shards(trailing, panel):
    rows, cols = lax.axis_size("prow"), lax.axis_size("pcol")
    if cols == 2 and rows == 4 * PLANE and panel.shape[1] % 128 == 0:
        return tuple(update(trailing, *fused(trailing, panel, rows)))
    gather = lambda value: lax.all_to_all(
        lax.all_gather(value, "prow", axis=0, tiled=True), "pcol", 0, 1, tiled=True
    )
    panel_rows = lax.all_gather(panel, "pcol", axis=1, tiled=True)
    panel_cols = gather(panel)
    gram = lax.psum(matmul(panel_cols.T, panel_cols), "pcol")
    factor = jnp.linalg.cholesky(gram)
    solve = functools.partial(
        lax.linalg.triangular_solve, factor, left_side=False, lower=True, transpose_a=True
    )
    basis_rows, basis_cols = solve(panel_rows), solve(panel_cols)
    part = lax.psum_scatter(
        matmul(trailing, basis_cols), "pcol", scatter_dimension=1, tiled=True
    )
    product_rows = lax.all_gather(part, "pcol", axis=1, tiled=True)
    product_cols = gather(part)
    projected = lax.psum(matmul(basis_cols.T, product_cols), "pcol")
    correction = product_rows - 0.5 * matmul(basis_rows, projected)
    correction_cols = product_cols - 0.5 * matmul(basis_cols, projected)
    updated = trailing - matmul(basis_rows, correction_cols.T) - matmul(correction, basis_cols.T)
    return (updated, basis_rows)


def solution(mesh):
    in_specs = (P("prow", "pcol"), P("prow", "pcol"))
    out_specs = (P("prow", "pcol"), P("prow", None))
    return jax.shard_map(shards, mesh=mesh, in_specs=in_specs, out_specs=out_specs, check_vma=False)
```

```python
import functools
import jax
import jax.numpy as jnp
from jax import lax
from jax.experimental import pallas as pl
from jax.experimental.pallas import tpu as pltpu
from jax.sharding import PartitionSpec as P

MESH = pl.DeviceIdType.MESH
SUB = 8
PLANE = 4
BLOCK = 128
CHUNKS = 1


def matmul(left, right):
    return jnp.dot(left, right, precision=lax.Precision.HIGHEST, preferred_element_type=jnp.float32)


def dot_exact(left, right, dims):
    return lax.dot_general(
        left, right, (dims, ((), ())), precision=lax.Precision.HIGHEST,
        preferred_element_type=jnp.float32,
    )


def split(value):
    high = value.astype(jnp.bfloat16)
    low = (value - high.astype(jnp.float32)).astype(jnp.bfloat16)
    return high, low


def dot_split(left, right, dims):
    dot = functools.partial(
        lax.dot_general, dimension_numbers=(dims, ((), ())), preferred_element_type=jnp.float32
    )
    (left_high, left_low), (right_high, right_low) = left, right
    return dot(left_high, right_high) + (dot(left_high, right_low) + dot(left_low, right_high))


NN = ((1,), (0,))
NT = ((1,), (1,))
TN = ((0,), (0,))


def factor_rows(index, lo, work, upper):
    hi = lo + upper.shape[1] // 2 + BLOCK
    start = pl.multiple_of(index * SUB, SUB)
    rows = work[pl.ds(start, SUB), lo:hi]
    lane = lax.broadcasted_iota(jnp.int32, (SUB, BLOCK), 1)
    sub = lax.broadcasted_iota(jnp.int32, (SUB, BLOCK), 0)
    diagonal = [
        jnp.broadcast_to(
            jnp.sum(jnp.where(lane == start - lo + i, rows[:, :BLOCK], 0.0), axis=1, keepdims=True),
            (SUB, BLOCK),
        )
        for i in range(SUB)
    ]
    unit = [jnp.where(sub == i, 1.0, 0.0).astype(jnp.float32) for i in range(SUB)]
    pivots = diagonal[0]
    for i in range(SUB):
        pivots = jnp.where(sub == i, diagonal[i], pivots)
        if i + 1 < SUB:
            pivot = jnp.broadcast_to(diagonal[i][i : i + 1, :], (SUB, BLOCK))
            ratio = jnp.where(sub > i, diagonal[i], 0.0) * pl.reciprocal(pivot)
            for k in range(i + 1, SUB):
                diagonal[k] = diagonal[k] - ratio * diagonal[k][i : i + 1, :]
            for k in range(i + 1):
                unit[k] = unit[k] - ratio * unit[k][i : i + 1, :]
    scale = lax.rsqrt(pivots)
    scale = scale * (1.5 - 0.5 * (pivots * scale) * scale)
    reduced = jnp.zeros_like(rows)
    for i in range(SUB):
        weight = jnp.concatenate([scale * unit[i]] * (rows.shape[1] // BLOCK), 1)
        reduced = reduced + weight * rows[i : i + 1, :]
    upper[pl.ds(start, SUB), lo:hi] = reduced
    high = reduced.astype(jnp.bfloat16).astype(jnp.float32)
    rest = reduced - high
    mid = rest.astype(jnp.bfloat16).astype(jnp.float32)
    low = rest - mid
    left = jnp.concatenate([part[:, :BLOCK] for part in (high, high, mid, high, low, mid)], 0)
    right = jnp.concatenate([high, mid, high, low, high, mid], 0)
    work[lo : lo + BLOCK, lo:hi] -= lax.dot_general(
        left.astype(jnp.bfloat16), right.astype(jnp.bfloat16), (TN, ((), ())),
        preferred_element_type=jnp.float32,
    )


def factor_below(lo, work, upper):
    width = upper.shape[1] // 2
    mid, hi = lo + BLOCK, lo + width + BLOCK
    if mid < width:
        work[mid:, mid:hi] -= dot_exact(upper[lo:mid, mid:width], upper[lo:mid, mid:hi], TN)


def kernel(planes, trailing, panel, pcols, wcols, rowside, basis_out, held, pblocks, wblocks,
           partial, wrecv, gram, grecv, proj, hrecv, work, upper, load_sem, store_sem, pz, p1, p2, ps, precv, psib, wz, w1, w2, ws, wr, wsib,
           swap_send, swap_recv):
    row, col = lax.axis_index("prow"), lax.axis_index("pcol")
    height, half = panel.shape
    width = 2 * half
    depth = row // PLANE
    place = lax.rem(row, PLANE)
    stride1 = 2 - col
    stride2 = 1 + col
    flip1 = stride1 * (1 - 2 * lax.rem(place // stride1, 2))
    flip2 = stride2 * (1 - 2 * lax.rem(place // stride2, 2))
    other = 1 - col
    near = planes // 2
    chunk = height // CHUNKS

    upper_half = depth // near
    mirrored = depth + upper_half * (planes - 1 - 2 * depth)

    def plane_of(k):
        plane = k + (1 - 2 * k) * mirrored if k < 2 else k
        return plane + upper_half * (planes - 1 - 2 * plane)

    load = pltpu.make_async_copy(trailing, held, load_sem)
    load.start()
    barrier = pltpu.get_barrier_semaphore()
    peers = [(plane_of(k) * PLANE + place, col) for k in range(1, planes)]
    peers += [(row + flip1, col), (row + flip2, col), (row, other)]
    for peer in peers:
        pl.semaphore_signal(barrier, inc=1, device_id=peer, device_id_type=MESH)
    pl.semaphore_wait(barrier, len(peers))

    class Gather:
        def __init__(self, blocks, sends, recv, sib):
            self.blocks, self.recv, self.sib = blocks, recv, sib
            self.sz, self.s1, self.s2, self.ss = sends

        def part(self, which, block, h):
            return self.blocks.at[which, block, pl.ds(h * chunk, chunk)]

        def copy(self, which, block, h, sem, recv, to):
            ref = self.part(which, block, h)
            return pltpu.make_async_remote_copy(
                src_ref=ref, dst_ref=ref, send_sem=sem, recv_sem=recv.at[block, h],
                device_id=to, device_id_type=MESH,
            )

        def zcopy(self, k, h):
            return self.copy(col, row, h, self.sz.at[k, h], self.recv,
                             (plane_of(k) * PLANE + place, col))

        def copy1(self, k, h):
            return self.copy(col, plane_of(k) * PLANE + place, h, self.s1.at[k, h], self.recv,
                             (row + flip1, col))

        def copy2(self, k, h, hop):
            return self.copy(col, plane_of(k) * PLANE + place + hop * flip1, h,
                             self.s2.at[k, hop, h], self.recv, (row + flip2, col))

        def copys(self, block, h):
            return self.copy(col, block, h, self.ss.at[block, h], self.sib, (row, other))

        def arrived(self, block, h):
            self.copy(col, block, h, self.sz.at[0, 0], self.recv, (row, other)).wait_recv()

        def sibling_arrived(self, block, h):
            self.copy(other, block, h, self.sz.at[0, 0], self.sib, (row, other)).wait_recv()

        def own_arrived(self):
            for h in range(CHUNKS):
                self.sibling_arrived(row, h)

        def first(self):
            for h in range(CHUNKS):
                self.copy1(0, h).start()
                self.copy2(0, h, 0).start()
                for k in range(1, planes):
                    self.zcopy(k, h).start()
            for h in range(CHUNKS):
                self.copys(row, h).start()

        def offset(self, k, i):
            return plane_of(k) * PLANE + place + lax.rem(i, 2) * flip1 + i // 2 * flip2

        def hand_over(self, k, h, i):
            @pl.when(plane_of(k) // near != col)
            def _():
                self.copys(self.offset(k, i), h).start()

        def forward0(self, k, h):
            self.arrived(self.offset(k, 0), h)
            self.copy1(k, h).start()
            self.copy2(k, h, 0).start()
            self.hand_over(k, h, 0)

        def forward1(self, k, h):
            self.arrived(self.offset(k, 1), h)
            self.copy2(k, h, 1).start()
            self.hand_over(k, h, 1)

        def forward2(self, k, h):
            for i in (2, 3):
                self.arrived(self.offset(k, i), h)
                self.hand_over(k, h, i)

        def steps(self, use):
            def pair(k, g):
                @pl.when(plane_of(k) // near == col)
                def _():
                    for i in (2 * g, 2 * g + 1):
                        for h in range(CHUNKS):
                            if k or i:
                                self.sibling_arrived(self.offset(k, i), h)

                    @pl.loop(2 * g, 2 * g + 2)
                    def _(i):
                        use(self.offset(k, i))

            items = [(k, h) for k in range(planes) for h in range(CHUNKS)]
            out, ready, waiting = [(self.own_arrived, ())], [], []
            for t in range(len(items) + 2):
                ready, waiting = ready + waiting, []
                for lag, step in ((0, self.forward0), (1, self.forward1), (2, self.forward2)):
                    if 0 <= t - lag < len(items):
                        k, h = items[t - lag]
                        if lag or k:
                            out.append((step, (k, h)))
                        if lag and h == CHUNKS - 1:
                            waiting.append((pair, (k, lag - 1)))
                out += ready[:1]
                ready = ready[1:]
            return out + ready + waiting

        def finish(self):
            for h in range(CHUNKS):
                self.copys(row, h).wait_send()
                for k in range(planes):
                    if k:
                        self.zcopy(k, h).wait_send()
                    self.copy1(k, h).wait_send()
                    for hop in range(2):
                        self.copy2(k, h, hop).wait_send()

                    @pl.when(plane_of(k) // near != col)
                    def _():
                        for i in range(PLANE):
                            if k or i:
                                self.copys(self.offset(k, i), h).wait_send()

    def full(blocks, block):
        return jnp.concatenate([blocks[0, block], blocks[1, block]], 1)

    def swap(source, target, slot):
        return pltpu.make_async_remote_copy(
            src_ref=source, dst_ref=target, send_sem=swap_send.at[slot],
            recv_sem=swap_recv.at[slot], device_id=(row, other), device_id_type=MESH,
        )

    pgather = Gather(pblocks, (pz, p1, p2, ps), precv, psib)
    pblocks[col, row] = panel[...]
    pgather.first()
    partial[...] = jnp.zeros_like(partial)
    gram[...] = jnp.zeros_like(gram)
    load.wait()

    def multiply(block):
        columns = pl.ds(pl.multiple_of((block - col * near * PLANE) * height, height), height)
        values = full(pblocks, block)
        product = dot_split(split(held[:, columns]), split(values), NN)
        partial[0] += product[:, :half]
        partial[1] += product[:, half:]
        gram[...] += dot_exact(values, values, TN)

    for step, at in pgather.steps(multiply):
        step(*at)

    wswap = swap(partial.at[other], wrecv, 0)
    wswap.start()
    gswap = swap(gram, grecv, 1)
    gswap.start()
    wswap.wait()
    wblocks[col, row] = partial[col] + wrecv[...]
    wgather = Gather(wblocks, (wz, w1, w2, ws), wr, wsib)
    wgather.first()
    gswap.wait()
    work[:, :width] = gram[...] + grecv[...]
    work[:, width:] = jnp.where(
        lax.broadcasted_iota(jnp.int32, (width, width), 0)
        == lax.broadcasted_iota(jnp.int32, (width, width), 1), 1.0, 0.0)

    upper[...] = jnp.zeros_like(upper)
    proj[...] = jnp.zeros_like(proj)
    mine = pl.ds(col * near * PLANE, near * PLANE)
    pstore = pltpu.make_async_copy(pblocks.at[:, mine], pcols, store_sem.at[0])
    pstore.start()

    def project(block):
        proj[...] += dot_exact(full(pblocks, block), full(wblocks, block), TN)

    wsteps = wgather.steps(project)
    count = BLOCK // SUB
    pieces = 8
    each = -(-len(wsteps) // (pieces * (width // BLOCK)))
    for lo in range(0, width, BLOCK):
        for piece in range(pieces):
            first, last = count * piece // pieces, count * (piece + 1) // pieces
            lax.fori_loop(lo // SUB + first, lo // SUB + last,
                          lambda j, _: (factor_rows(j, lo, work, upper), 0)[1], 0)
            for step, at in wsteps[:each]:
                step(*at)
            wsteps = wsteps[each:]
        factor_below(lo, work, upper)

    linv = upper[:, width:]
    basis = dot_exact(full(pblocks, row), linv, NT)
    basis_out[...] = basis
    rowside[:, :width] = dot_exact(basis, linv, NN)
    solved = dot_exact(dot_exact(full(wblocks, row), linv, NT), linv, NN)
    work[:, :width] = dot_exact(linv, linv, TN)
    for step, at in wsteps:
        step(*at)
    hswap = swap(proj, hrecv, 2)
    hswap.start()
    wstore = pltpu.make_async_copy(wblocks.at[:, mine], wcols, store_sem.at[1])
    wstore.start()
    hswap.wait()
    total = proj[...] + hrecv[...]
    rowside[:, width:] = solved - dot_exact(
        rowside[:, :width], dot_exact(total, work[:, :width], NN), NN
    )
    pgather.finish()
    wgather.finish()
    pstore.wait()
    wstore.wait()


def update_kernel(trailing, pcols, wcols, rowside, basis, updated, basis_out, left, right):
    depth = rowside.shape[1]

    @pl.when(pl.program_id(0) == 0)
    def _():
        high, low = split(rowside[...])
        left[:, :depth], left[:, depth : 2 * depth], left[:, 2 * depth :] = high, high, low
        basis_out[...] = basis[...]

    for i, ref in enumerate((wcols, pcols)):
        for j in range(2):
            half = ref.shape[3]
            high, low = split(ref[j, 0])
            for part, value in enumerate((high, low, high)):
                start = part * depth + (2 * i + j) * half
                right[:, start : start + half] = value
    updated[...] = trailing[...] - lax.dot_general(
        left[...], right[...], (NT, ((), ())), preferred_element_type=jnp.float32
    )


def update(trailing, pcols, wcols, rowside, basis):
    height, width = basis.shape
    _, blocks, _, half = pcols.shape
    square = pl.BlockSpec((height, height), lambda j: (0, j))
    column = pl.BlockSpec((2, 1, height, half), lambda j: (0, j, 0, 0))
    whole = lambda *shape: pl.BlockSpec(shape, lambda j: (0, 0))
    return pl.pallas_call(
        update_kernel,
        grid=(blocks,),
        out_shape=(jax.ShapeDtypeStruct(trailing.shape, jnp.float32),
                   jax.ShapeDtypeStruct(basis.shape, jnp.float32)),
        in_specs=[square, column, column, whole(height, 2 * width), whole(height, width)],
        out_specs=[square, whole(height, width)],
        scratch_shapes=[pltpu.VMEM((height, 6 * width), jnp.bfloat16)] * 2,
        compiler_params=pltpu.CompilerParams(vmem_limit_bytes=60 * 2**20),
        name="update",
    )(trailing, pcols, wcols, rowside, basis)


def fused(trailing, panel, rows):
    height, half = panel.shape
    width = 2 * half
    planes = rows // PLANE
    blocks = (2, rows, height, half)
    dma = pltpu.SemaphoreType.DMA
    vmem = lambda *shape: pltpu.VMEM(shape, jnp.float32)
    gather_sems = [dma((planes, CHUNKS)), dma((planes, CHUNKS)), dma((planes, 2, CHUNKS)),
                   dma((rows, CHUNKS)), dma((rows, CHUNKS)), dma((rows, CHUNKS))]
    return pl.pallas_call(
        functools.partial(kernel, planes),
        out_shape=tuple(jax.ShapeDtypeStruct(shape, jnp.float32) for shape in (
            (2, rows // 2, height, half), (2, rows // 2, height, half), (height, 2 * width),
            (height, width))),
        in_specs=[pl.BlockSpec(memory_space=pl.ANY), pl.BlockSpec(memory_space=pltpu.VMEM)],
        out_specs=[pl.BlockSpec(memory_space=pl.ANY)] * 2
        + [pl.BlockSpec(memory_space=pltpu.VMEM)] * 2,
        scratch_shapes=[
            vmem(*trailing.shape), vmem(*blocks), vmem(*blocks), vmem(2, height, half),
            vmem(height, half), vmem(width, width), vmem(width, width), vmem(width, width),
            vmem(width, width), vmem(width, 2 * width), vmem(width, 2 * width),
            dma, dma((2,)), *gather_sems, *gather_sems, dma((3,)), dma((3,)),
        ],
        compiler_params=pltpu.CompilerParams(
            collective_id=0, has_side_effects=True, vmem_limit_bytes=56 * 2**20
        ),
        name="panel_update",
    )(trailing, panel)


def shards(trailing, panel):
    rows, cols = lax.axis_size("prow"), lax.axis_size("pcol")
    if cols == 2 and rows == 4 * PLANE and panel.shape[1] % 128 == 0:
        return tuple(update(trailing, *fused(trailing, panel, rows)))
    gather = lambda value: lax.all_to_all(
        lax.all_gather(value, "prow", axis=0, tiled=True), "pcol", 0, 1, tiled=True
    )
    panel_rows = lax.all_gather(panel, "pcol", axis=1, tiled=True)
    panel_cols = gather(panel)
    gram = lax.psum(matmul(panel_cols.T, panel_cols), "pcol")
    factor = jnp.linalg.cholesky(gram)
    solve = functools.partial(
        lax.linalg.triangular_solve, factor, left_side=False, lower=True, transpose_a=True
    )
    basis_rows, basis_cols = solve(panel_rows), solve(panel_cols)
    part = lax.psum_scatter(
        matmul(trailing, basis_cols), "pcol", scatter_dimension=1, tiled=True
    )
    product_rows = lax.all_gather(part, "pcol", axis=1, tiled=True)
    product_cols = gather(part)
    projected = lax.psum(matmul(basis_cols.T, product_cols), "pcol")
    correction = product_rows - 0.5 * matmul(basis_rows, projected)
    correction_cols = product_cols - 0.5 * matmul(basis_cols, projected)
    updated = trailing - matmul(basis_rows, correction_cols.T) - matmul(correction, basis_cols.T)
    return (updated, basis_rows)


def solution(mesh):
    in_specs = (P("prow", "pcol"), P("prow", "pcol"))
    out_specs = (P("prow", "pcol"), P("prow", None))
    return jax.shard_map(shards, mesh=mesh, in_specs=in_specs, out_specs=out_specs, check_vma=False)
```
